128 devices in a mesh: dp: 8 (over x, core), fsdp: 16 (over z, y).
Axes of the slice: x: 4, y: 4, z: 4, core: 2. Of those that a mesh axis runs over, the one named last changes fastest.
Arguments:
- context: bfloat16 [65536, 8192], P(('dp', 'fsdp')), may hold values from -24 to 24
- cotangent: bfloat16 [65536, 1024], P(('dp', 'fsdp')), may hold values from -6 to 6
- out_weight: bfloat16 [8192, 1024], P('fsdp'), may hold values from -0.0625 to 0.0625
- error_memory: bfloat16 [8, 8192, 1024], P('dp', 'fsdp'), may hold values from -30 to 30, as said below
- seed_factor: float32 [4, 1024], replicated, may hold values from -0.1875 to 0.1875
Outputs:
- context_grad: bfloat16 [65536, 8192], P(('dp', 'fsdp'))
- new_memory: bfloat16 [8, 8192, 1024], P('dp', 'fsdp')
- right_factor: float32 [4, 1024], replicated
The draws below stay inside these ranges and needn't reach their ends.
Inputs may be any that keep to these rules, and one draw needn't show every extreme that they name: `error_memory`: entries of the error memories.
All inputs are finite; a program needn't handle non-finite values.
Results may differ from the reference program's by a relative error of at most 0.011.
Values may be sent and summed in bfloat16 or wider, within the bound.
A program may use at most 128 MiB of HBM per device.

```python
import jax
import jax.numpy as jnp
from jax import lax

D = 1024
RANK = 4
TOK_DEV = 512
INNER = 8192
TOKENS = 65536
N_DP = 8
N_FSDP = 16


def draw_error_memory(key, part):
    key = jax.random.fold_in(key, 11)
    position = jnp.arange(INNER, dtype=jnp.float32) / INNER
    row_scale = 0.5 * jnp.power(10.0, position)
    values = jnp.clip(jax.random.normal(key, (N_DP, INNER, D), jnp.float32), -6.0, 6.0)
    return (values * row_scale[None, :, None]).astype(jnp.bfloat16)


def with_spikes(result, own_key, source, target, shards_of, factor):
    owner, partner = [(jnp.arange(result.shape[dim]) // (result.shape[dim] // shards_of)).reshape([-1 if axis == dim else 1 for axis in range(result.ndim)]) for dim in (source, target)]
    chosen = jax.random.permutation(own_key, shards_of)[partner]
    strong = (owner == chosen) | (owner == (partner + shards_of // 2) % shards_of)
    return jnp.where(strong, factor * result, result)


def level_of(key, shape, split, least, high):
    level = 1.0
    for axis_at, shards_of in split:
        steps = jax.random.uniform(jax.random.fold_in(jax.random.fold_in(key, 6), axis_at), (shards_of,), jnp.float32, least / len(split), high / len(split))
        level = level * jnp.repeat(jnp.exp(steps), shape[axis_at] // shards_of).reshape((-1,) + (1,) * (len(shape) - 1 - axis_at))
    return level


def bell_draw(key, shape, width, bound, cuts=(), held_as=jnp.bfloat16):
    gain = level_of(key, shape, cuts, -0.22, 0.18) if cuts else 1.0
    entries = jax.random.normal(key, shape, jnp.float32) * width * gain
    return jnp.minimum(jnp.maximum(entries, -bound), bound).astype(held_as)


def gaussian_with(rng, shape, spread, bound, split, heavy, kind=jnp.bfloat16):
    array = spread * jax.random.normal(rng, shape, jnp.float32)
    if split:
        array = array * level_of(rng, shape, split, -0.22, 0.18)
    return jnp.clip(with_spikes(array, jax.random.fold_in(rng, 3), *heavy), -bound, bound).astype(kind)


def setup_inputs(seed: int = 0) -> dict:
    seeds = jax.random.split(jax.random.key(seed), 6)
    context = gaussian_with(seeds[0], (TOKENS, INNER), 1.0, 24.0, ((0, 128),), (0, 1, 128, 5.5))
    cotangent = bell_draw(seeds[1], (TOKENS, D), 1.0, 6.0, ((0, 128),))
    out_weight = bell_draw(seeds[2], (INNER, D), INNER ** -0.5, 0.0625, ((0, 16),))
    error_memory = draw_error_memory(jax.random.fold_in(seeds[5], 71), 0)
    seed_factor = bell_draw(seeds[4], (RANK, D), D ** -0.5, 0.1875, (), jnp.float32)
    return dict(context=context, cotangent=cotangent, out_weight=out_weight, error_memory=error_memory, seed_factor=seed_factor)


EPSILON = 1e-06
HIGH = lax.Precision.HIGHEST

def orthonormal(factor_rows):
    basis = []
    for column in range(RANK):
        vector = factor_rows[column]
        if column > 0:
            stacked = jnp.stack(basis)
            coeffs = jnp.dot(stacked, vector, precision=HIGH)
            vector = vector - jnp.dot(coeffs, stacked, precision=HIGH)
        length = jnp.sqrt(jnp.sum(vector * vector) + EPSILON)
        basis.append(vector / length)
    return jnp.stack(basis)

def reference(context, cotangent, out_weight, error_memory, seed_factor):
    context_grad = lax.dot_general(cotangent, out_weight, (((1,), (1,)), ((), ())), preferred_element_type=jnp.float32).astype(jnp.bfloat16)
    group_tokens = TOK_DEV * N_FSDP
    scale = 1.0 / jnp.sqrt(jnp.float32(group_tokens))

    def group_memory(index):
        ctx_block = lax.dynamic_slice_in_dim(context, index * group_tokens, group_tokens, 0)
        cot_block = lax.dynamic_slice_in_dim(cotangent, index * group_tokens, group_tokens, 0)
        total = jnp.zeros((INNER, D), jnp.float32)
        for block in range(N_FSDP):
            ctx_part = ctx_block[block * TOK_DEV:(block + 1) * TOK_DEV]
            cot_part = cot_block[block * TOK_DEV:(block + 1) * TOK_DEV]
            term = lax.dot_general(ctx_part, cot_part, (((0,), (0,)), ((), ())), preferred_element_type=jnp.float32)
            total = total + term.astype(jnp.bfloat16).astype(jnp.float32)
        memory_one = lax.dynamic_index_in_dim(error_memory, index, 0, False)
        return total * scale + memory_one.astype(jnp.float32)
    memory = lax.map(group_memory, jnp.arange(N_DP, dtype=jnp.int32))
    left_terms = lax.map(lambda matrix: lax.dot_general(seed_factor, matrix, (((1,), (1,)), ((), ())), precision=HIGH), memory)
    p_sum = lax.optimization_barrier(jnp.sum(left_terms, axis=0))
    p_hat = orthonormal(p_sum)
    right_terms = lax.map(lambda matrix: jnp.dot(p_hat, matrix, precision=HIGH), memory)
    right_factor = lax.optimization_barrier(jnp.sum(right_terms, axis=0)) / N_DP
    approx = lax.dot_general(p_hat, right_factor, (((0,), (0,)), ((), ())), precision=HIGH)
    new_memory = (memory - approx[None]).astype(jnp.bfloat16)
    return (context_grad, new_memory, right_factor)
```

```python
import functools

import jax
import jax.numpy as jnp
import numpy as np
from jax import lax
from jax.experimental import pallas as pl
from jax.experimental.pallas import tpu as pltpu
from jax.sharding import PartitionSpec as P

MESH = pl.DeviceIdType.MESH
F32 = jnp.float32
BF16 = jnp.bfloat16
EPSILON = 1e-06
TOK = 512
CH = 512
D = 1024
N_DP = 8
N_FSDP = 16
PIECE = 128
HALF = 512
SCALE = float(np.float32(1.0) / np.sqrt(np.float32(TOK * N_FSDP)))
EXCHANGE_ORDER = (0, 1, 4, 2, 5, 3, 6, 7)


def dot_tn(a, b):
    return lax.dot_general(a, b, (((0,), (0,)), ((), ())), preferred_element_type=F32)


def dot_nn(a, b):
    return lax.dot_general(a, b, (((1,), (0,)), ((), ())), preferred_element_type=F32)


def dot_nt(a, b):
    return lax.dot_general(a, b, (((1,), (1,)), ((), ())), preferred_element_type=F32)


def parts(v):
    hi = v.astype(BF16).astype(F32)
    rest = v - hi
    mid = rest.astype(BF16).astype(F32)
    return hi, mid, rest - mid


def stack(v):
    hi, mid, lo = parts(v)
    return jnp.concatenate([hi, mid, lo, jnp.zeros_like(hi)], axis=0).astype(BF16)


def fold(r):
    return r[0:8] + (r[8:16] + r[16:24])


def xor2(a, m):
    return ((a // 2 + m // 2) % 2) * 2 + (a % 2 + m % 2) % 2


def mask_of(i):
    return ((i + 1) % 3 + 1) * ((i + 2) // 3)


def kernel(
    seed_ref, cot_h, ctx_h, w_h, err_h,
    grad_h, newmem_ref, right_ref,
    ctx_v, cot_v, err_v, cotp, ctxp, s1s, s1r, rsend, opp, fin, wg, stage, base,
    ppart, rb1, rb2, rb3, pall, phat, rb5, rb6, rb7,
    lsem, osem, ssem, rsem,
):
    dp, fs = lax.axis_index("dp"), lax.axis_index("fsdp")
    x, c = dp // 2, dp % 2
    z, y = fs // 4, fs % 4
    a, b = z * (1 - c) + y * c, y * (1 - c) + z * c

    def fid(i, j):
        return (i * (1 - c) + j * c) * 4 + j * (1 - c) + i * c

    def at(i, j):
        return (dp, fid(i, j))

    aA, aB, bA, bB = xor2(a, 1), 3 - a, xor2(b, 1), 3 - b
    bP, bM = (b + 1) % 4, (b + 3) % 4
    xR, xL, xO = (x + 1) % 4, (x + 3) % 4, (x + 2) % 4
    right_chip, left_chip = (xR * 2 + c, fs), (xL * 2 + c, fs)
    sibling = (x * 2 + 1 - c, fs)
    border = [(b + k) % 4 for k in (2, 1, 3, 0)]
    row8 = lax.broadcasted_iota(jnp.int32, (8, CH), 0)

    cot_load = pltpu.make_async_copy(cot_h, cot_v, lsem.at[0])
    cot_load.start()
    for f in range(N_FSDP):
        pltpu.make_async_copy(ctx_h.at[:, pl.ds(f * CH, CH)], ctx_v.at[f], lsem.at[1]).start()
    err_load = pltpu.make_async_copy(err_h, err_v, lsem.at[2])
    err_load.start()
    my_rows, my_cols = pl.ds(pl.multiple_of(x * PIECE, PIECE), PIECE), pl.ds(pl.multiple_of(c * HALF, HALF), HALF)
    w_load = pltpu.make_async_copy(w_h.at[my_rows, my_cols], wg.at[a * 4 + b, my_rows, my_cols], lsem.at[3])
    w_load.start()

    barrier = pltpu.get_barrier_semaphore()
    peers = [((dp + i) % N_DP, fs) for i in range(1, N_DP)]
    peers += [(dp, ((z + i) % 4) * 4 + y) for i in range(1, 4)]
    peers += [(dp, z * 4 + (y + i) % 4) for i in range(1, 4)]
    for peer in peers:
        pl.semaphore_signal(barrier, inc=1, device_id=peer, device_id_type=MESH)
    pl.semaphore_wait(barrier, len(peers))

    sent = []

    def send(src, dst, device):
        n = len(sent)
        copy = pltpu.make_async_remote_copy(src, dst, ssem.at[n], rsem.at[n], device_id=device, device_id_type=MESH)
        copy.start()
        sent.append(copy)
        return copy

    def wslice(first, count, slot, core):
        return wg.at[
            pl.ds(first, count),
            pl.ds(pl.multiple_of(slot * PIECE, PIECE), PIECE),
            pl.ds(pl.multiple_of(core * HALF, HALF), HALF),
        ]

    def dp_exchange(src_of, buf):
        return [send(src_of((dp + i) % N_DP), buf.at[dp], ((dp + i) % N_DP, fs)) for i in range(1, N_DP)]

    def z_exchange(buf):
        return [send(buf.at[z], buf.at[z], (dp, ((z + i) % 4) * 4 + y)) for i in range(1, 4)]

    def y_exchange(buf):
        return [send(buf.at[y], buf.at[y], (dp, z * 4 + (y + i) % 4)) for i in range(1, 4)]

    def arrive(copies):
        for copy in copies:
            copy.wait_recv()

    def total(buf, n):
        t = buf[0]
        for i in range(1, n):
            t = t + buf[i]
        return t

    def product(f, j):
        return dot_tn(ctx_v[f], cot_v[...]) + dot_tn(ctxp[j], cotp[...])

    exchange = {}

    def send_columns(step):
        j = EXCHANGE_ORDER[step]
        owner = 3 - aA if j < 4 else aA
        exchange[j] = send(ctx_v.at[fid(owner, border[j % 4])], ctxp.at[j], at(aA, b))

    first = {}

    def make_first(k):
        exchange[k].wait_recv()
        s1s[k] = product(fid(aB, border[k]), k).astype(BF16)

    def send_first(k, half):
        rows = pl.ds(half * 256, 256)
        first[k, half] = send(s1s.at[k, rows], s1r.at[k, rows], at(aB, b))

    second = {}

    def make_second(k):
        exchange[4 + k].wait_recv()
        first[k, 0].wait_recv()
        first[k, 1].wait_recv()
        rsend[k] = (product(fid(a, border[k]), 4 + k) + s1r[k].astype(F32)).astype(BF16)

    low, high = pl.ds(0, 256), pl.ds(256, 256)

    ring = {}

    def group(i):
        return xor2(a, int(mask_of(i)))

    def x_own(i, part):
        src = wslice(group(i) * 4 + part * 2, 2, x, c)
        ring[i, part, "right"] = send(src, src, right_chip)
        ring[i, part, "left"] = send(src, src, left_chip)

    def x_forward(i):
        ring[i, 0, "right"].wait_recv()
        ring[i, 1, "left"].wait_recv()
        src = wslice(group(i) * 4, 2, xL, c)
        ring[i, 2, "right"] = send(src, src, right_chip)
        src = wslice(group(i) * 4 + 2, 2, xR, c)
        ring[i, 2, "left"] = send(src, src, left_chip)

    across = {}

    def x_finish(i):
        ring[i, 0, "left"].wait_recv()
        ring[i, 1, "right"].wait_recv()
        ring[i, 2, "right"].wait_recv()
        ring[i, 2, "left"].wait_recv()
        across[i] = [
            send(wg.at[group(i) * 4 + j, :, my_cols], wg.at[j * 4 + group(i), :, my_cols], sibling) for j in range(4)
        ]

    def out_copy(slot, f):
        return pltpu.make_async_copy(
            stage.at[slot], grad_h.at[:, pl.ds(pl.multiple_of(f * CH, CH), CH)], osem.at[slot]
        )

    def multiply(i):
        arrive(across[i])

        def step(t, carry):
            n = i * i + t
            slot = n % 2
            ga = xor2(a, mask_of(jnp.minimum(t, i)))
            gb = xor2(b, mask_of(jnp.minimum(i, 2 * i - t)))

            @pl.when(n >= 2)
            def _():
                out_copy(slot, 0).wait()

            stage[slot] = dot_nt(cot_v[...], wg[ga * 4 + gb]).astype(BF16)
            out_copy(slot, fid(ga, gb)).start()
            return carry

        lax.fori_loop(0, 2 * i + 1, step, 0)

    cot_sent = send(cot_h, cotp, at(aA, b))
    w_load.wait()
    own = wslice(a * 4 + b, 1, x, c)
    w_a = send(own, own, at(a, bA))
    w_b = send(own, own, at(a, bB))

    cot_load.wait()
    seed32 = stack(seed_ref[...])
    q32 = stack(fold(dot_nt(seed32, cot_v[...])))
    pltpu.make_async_copy(ctx_v, ctx_v, lsem.at[1]).wait()

    def left_terms(s, carry):
        even = fold(dot_nn(q32, ctx_v[2 * s]))
        odd = fold(dot_nn(q32, ctx_v[2 * s + 1]))
        ppart[s] = jnp.where(row8 < 4, even, odd) * SCALE
        return carry

    lax.fori_loop(0, N_DP, left_terms, 0)
    err_load.wait()
    err_term = fold(dot_nt(seed32, err_v[...]))
    mine8 = (row8 // 4) == (fs % 2)
    ppart[fs // 2] = ppart[fs // 2] + jnp.where(mine8, err_term, 0.0)

    rb1[dp] = ppart[dp]
    ph1 = dp_exchange(lambda peer: ppart.at[peer], rb1)
    w_a.wait_recv()
    src = wslice(a * 4 + bA, 1, x, c)
    w_f = send(src, src, at(a, bB))
    w_b.wait_recv()
    arrive(ph1)
    rb2[z] = total(rb1, N_DP)
    ph2 = z_exchange(rb2)

    send_columns(0)
    w_f.wait_recv()
    src = wslice(a * 4, 4, x, c)
    g_b = send(src, src, at(aB, b))
    x_own(0, 0)
    arrive(ph2)
    rb3[y] = total(rb2, 4)
    ph3 = y_exchange(rb3)

    send_columns(1)
    x_own(0, 1)
    arrive(ph3)
    pall[dp] = total(rb3, 4)
    ph4 = dp_exchange(lambda peer: pall.at[dp], pall)

    send_columns(2)
    cot_sent.wait_recv()
    make_first(0)
    send_first(0, 0)
    x_forward(0)
    send_first(0, 1)
    arrive(ph4)

    send_columns(3)
    g_b.wait_recv()
    x_own(1, 0)

    def inner(u, v):
        t = u[0] * v[0] + u[1] * v[1]
        return jnp.sum(jnp.sum(t, axis=1, keepdims=True), axis=0, keepdims=True)

    basis = []
    for j in range(4):
        v = (pall[:, j, :], pall[:, j + 4, :])
        if j:
            coeffs = [inner(q, v) for q in basis]
            cut0 = coeffs[0] * basis[0][0]
            cut1 = coeffs[0] * basis[0][1]
            for k in range(1, j):
                cut0 = cut0 + coeffs[k] * basis[k][0]
                cut1 = cut1 + coeffs[k] * basis[k][1]
            v = (v[0] - cut0, v[1] - cut1)
        length = jnp.sqrt(inner(v, v) + EPSILON)
        v = (v[0] / length, v[1] / length)
        basis.append(v)
        phat[:, j, :] = v[0]
        phat[:, j + 4, :] = v[1]

    def rows_terms(s, carry):
        p32 = stack(phat[s])
        return carry[0] + dot_nt(p32, ctx_v[2 * s]), carry[1] + dot_nt(p32, ctx_v[2 * s + 1])

    zero = jnp.zeros((32, TOK), F32)
    even, odd = lax.fori_loop(0, N_DP, rows_terms, (zero, zero))
    mix = jnp.where(row8 < 4, fold(even), fold(odd))
    h8 = mix + jnp.concatenate([mix[4:8], mix[0:4]], axis=0)
    slot_rows = phat[fs // 2]
    turned = jnp.concatenate([slot_rows[4:8], slot_rows[0:4]], axis=0)
    p8 = jnp.where(mine8, slot_rows, turned)
    r8 = fold(dot_nn(stack(h8), cot_v[...])) * SCALE + fold(dot_nn(stack(p8), err_v[...]))
    rb5[dp] = jnp.where(row8 < 4, r8[:, 0:512], r8[:, 512:1024])
    ph5 = dp_exchange(lambda peer: rb5.at[dp], rb5)

    make_first(1)
    send_first(1, 0)
    send_columns(4)
    x_own(1, 1)
    arrive(ph5)
    rb6[z] = total(rb5, N_DP)
    ph6 = z_exchange(rb6)

    send_first(1, 1)
    send_columns(5)
    make_second(0)
    opp_low = send(rsend.at[0, low], opp.at[0], at(a, bP))
    opp_high = send(rsend.at[0, high], opp.at[1], at(a, bM))
    x_forward(1)
    arrive(ph6)
    rb7[y] = total(rb6, 4)
    ph7 = y_exchange(rb7)

    src = wslice(a * 4, 4, x, c)
    g_a = send(src, src, at(aA, b))
    make_first(2)
    send_first(2, 0)
    send_columns(6)
    arrive(ph7)
    factor = total(rb7, 4) * (1.0 / N_DP)
    right_ref[:, 0:512] = factor[0:4]
    right_ref[:, 512:1024] = factor[4:8]
    send_first(2, 1)
    send_columns(7)
    ph, pm, plo = parts(p8)
    rh, rm, rl = parts(factor)
    lhs = jnp.concatenate([ph, ph, pm, ph, plo, pm], axis=0).astype(BF16)
    rhs = jnp.concatenate([rh, rm, rh, rl, rh, rm], axis=0)
    row48 = lax.broadcasted_iota(jnp.int32, rhs.shape, 0) % 8
    rhs = jnp.concatenate([jnp.where(row48 < 4, rhs, 0.0), jnp.where(row48 >= 4, rhs, 0.0)], axis=1).astype(BF16)
    base[...] = err_v[...].astype(F32) - dot_tn(lhs, rhs)

    make_second(1)
    direct_r = send(rsend.at[1, high], fin.at[0, high], at(a, bP))
    g_a.wait_recv()
    src = wslice(aA * 4, 4, x, c)
    g_f = send(src, src, at(aB, b))
    x_own(2, 0)
    x_own(2, 1)
    make_first(3)
    send_first(3, 0)
    send_first(3, 1)
    opp_low.wait_recv()
    rsend[1, low] = (rsend[1, low].astype(F32) + opp[0].astype(F32)).astype(BF16)
    through_r = send(rsend.at[1, low], fin.at[0, low], at(a, bP))
    x_finish(0)
    multiply(0)
    make_second(2)
    direct_l = send(rsend.at[2, low], fin.at[1, low], at(a, bM))
    opp_high.wait_recv()
    rsend[2, high] = (rsend[2, high].astype(F32) + opp[1].astype(F32)).astype(BF16)
    through_l = send(rsend.at[2, high], fin.at[1, high], at(a, bM))
    g_f.wait_recv()
    x_own(3, 0)
    x_own(3, 1)
    x_finish(1)
    x_forward(2)
    exchange[7].wait_recv()
    base[...] += product(fid(a, b), 7) * SCALE
    multiply(1)
    x_finish(2)
    x_forward(3)
    multiply(2)

    for half, rows, copies in (
        (0, low, (first[3, 0], through_r, direct_l)),
        (1, high, (first[3, 1], direct_r, through_l)),
    ):
        arrive(copies)
        gathered = s1r[3, rows].astype(F32) + (fin[0, rows].astype(F32) + fin[1, rows].astype(F32))
        newmem_ref[rows, :] = (base[rows, :] + gathered * SCALE).astype(BF16)

    x_finish(3)
    multiply(3)
    out_copy(0, 0).wait()
    out_copy(1, 0).wait()
    for copy in sent:
        copy.wait_send()


N_SEMS = 160


def shards(context, cotangent, out_weight, error_memory, seed_factor):
    vmem, hbm = pl.BlockSpec(memory_space=pltpu.VMEM), pl.BlockSpec(memory_space=pl.ANY)
    seed8 = jnp.concatenate([seed_factor, seed_factor], axis=0)
    small = pltpu.VMEM((8, 8, 512), F32)
    quad = pltpu.VMEM((4, 8, 512), F32)
    context_grad, new_memory, right_factor = pl.pallas_call(
        kernel,
        out_shape=(
            jax.ShapeDtypeStruct((TOK, CH * N_FSDP), BF16),
            jax.ShapeDtypeStruct((CH, D), BF16),
            jax.ShapeDtypeStruct((4, D), F32),
        ),
        in_specs=[vmem, hbm, hbm, hbm, hbm],
        out_specs=(hbm, vmem, vmem),
        scratch_shapes=[
            pltpu.VMEM((N_FSDP, TOK, CH), BF16),
            pltpu.VMEM((TOK, D), BF16),
            pltpu.VMEM((CH, D), BF16),
            pltpu.VMEM((TOK, D), BF16),
            pltpu.VMEM((8, TOK, CH), BF16),
            pltpu.VMEM((4, CH, D), BF16),
            pltpu.VMEM((4, CH, D), BF16),
            pltpu.VMEM((3, CH, D), BF16),
            pltpu.VMEM((2, 256, D), BF16),
            pltpu.VMEM((2, CH, D), BF16),
            pltpu.VMEM((N_FSDP, CH, D), BF16),
            pltpu.VMEM((2, TOK, CH), BF16),
            pltpu.VMEM((CH, D), F32),
            small, small, quad, quad, small, small, small, quad, quad,
            pltpu.SemaphoreType.DMA((4,)),
            pltpu.SemaphoreType.DMA((2,)),
            pltpu.SemaphoreType.DMA((N_SEMS,)),
            pltpu.SemaphoreType.DMA((N_SEMS,)),
        ],
        compiler_params=pltpu.CompilerParams(
            collective_id=0, has_side_effects=True, vmem_limit_bytes=60 * 2**20
        ),
        cost_estimate=pl.CostEstimate(flops=18 * 2**30, bytes_accessed=20 * 2**20, transcendentals=0),
        name="projection_gradient",
    )(seed8, cotangent, context, out_weight, error_memory[0])
    return context_grad, new_memory[None], right_factor


def solution(mesh):
    placed = (
        P(("dp", "fsdp"), None),
        P(("dp", "fsdp"), None),
        P("fsdp", None),
        P("dp", "fsdp", None),
        P(),
    )
    return jax.shard_map(
        shards,
        mesh=mesh,
        in_specs=placed,
        out_specs=(P(("dp", "fsdp"), None), P("dp", "fsdp", None), P()),
        check_vma=False,
    )
```

```python
import functools

import jax
import jax.numpy as jnp
import numpy as np
from jax import lax
from jax.experimental import pallas as pl
from jax.experimental.pallas import tpu as pltpu
from jax.sharding import PartitionSpec as P

MESH = pl.DeviceIdType.MESH
F32 = jnp.float32
BF16 = jnp.bfloat16
EPSILON = 1e-06
TOK = 512
CH = 512
D = 1024
N_DP = 8
N_FSDP = 16
PIECE = 128
HALF = 512
SCALE = float(np.float32(1.0) / np.sqrt(np.float32(TOK * N_FSDP)))
EXCHANGE_ORDER = (0, 1, 4, 2, 5, 3, 6, 7)


def dot_tn(a, b):
    return lax.dot_general(a, b, (((0,), (0,)), ((), ())), preferred_element_type=F32)


def dot_nn(a, b):
    return lax.dot_general(a, b, (((1,), (0,)), ((), ())), preferred_element_type=F32)


def dot_nt(a, b):
    return lax.dot_general(a, b, (((1,), (1,)), ((), ())), preferred_element_type=F32)


def parts(v):
    hi = v.astype(BF16).astype(F32)
    rest = v - hi
    mid = rest.astype(BF16).astype(F32)
    return hi, mid, rest - mid


def stack(v):
    hi, mid, lo = parts(v)
    return jnp.concatenate([hi, mid, lo, jnp.zeros_like(hi)], axis=0).astype(BF16)


def fold(r):
    return r[0:8] + (r[8:16] + r[16:24])


def xor2(a, m):
    return ((a // 2 + m // 2) % 2) * 2 + (a % 2 + m % 2) % 2


def mask_of(i):
    return ((i + 1) % 3 + 1) * ((i + 2) // 3)


def kernel(
    seed_ref, cot_h, ctx_h, w_h, err_h,
    grad_ref, newmem_ref, right_ref,
    ctx_v, cot_v, err_v, cotp, ctxp, s1s, s1r, rsend, opp, fin, wg, base,
    ppart, rb1, rb2, rb3, pall, phat, rb5, rb6, rb7,
    lsem, ssem, rsem,
):
    dp, fs = lax.axis_index("dp"), lax.axis_index("fsdp")
    x, c = dp // 2, dp % 2
    z, y = fs // 4, fs % 4
    a, b = z * (1 - c) + y * c, y * (1 - c) + z * c

    def fid(i, j):
        return (i * (1 - c) + j * c) * 4 + j * (1 - c) + i * c

    def at(i, j):
        return (dp, fid(i, j))

    aA, aB, bA, bB = xor2(a, 1), 3 - a, xor2(b, 1), 3 - b
    bP, bM = (b + 1) % 4, (b + 3) % 4
    xR, xL, xO = (x + 1) % 4, (x + 3) % 4, (x + 2) % 4
    right_chip, left_chip = (xR * 2 + c, fs), (xL * 2 + c, fs)
    sibling = (x * 2 + 1 - c, fs)
    border = [(b + k) % 4 for k in (2, 1, 3, 0)]
    row8 = lax.broadcasted_iota(jnp.int32, (8, CH), 0)

    cot_load = pltpu.make_async_copy(cot_h, cot_v, lsem.at[0])
    cot_load.start()
    for f in range(N_FSDP):
        pltpu.make_async_copy(ctx_h.at[:, pl.ds(f * CH, CH)], ctx_v.at[f], lsem.at[1]).start()
    err_load = pltpu.make_async_copy(err_h, err_v, lsem.at[2])
    err_load.start()
    my_rows, my_cols = pl.ds(pl.multiple_of(x * PIECE, PIECE), PIECE), pl.ds(pl.multiple_of(c * HALF, HALF), HALF)
    w_load = pltpu.make_async_copy(w_h.at[my_rows, my_cols], wg.at[a * 4 + b, my_rows, my_cols], lsem.at[3])
    w_load.start()

    barrier = pltpu.get_barrier_semaphore()
    peers = [((dp + i) % N_DP, fs) for i in range(1, N_DP)]
    peers += [(dp, ((z + i) % 4) * 4 + y) for i in range(1, 4)]
    peers += [(dp, z * 4 + (y + i) % 4) for i in range(1, 4)]
    for peer in peers:
        pl.semaphore_signal(barrier, inc=1, device_id=peer, device_id_type=MESH)
    pl.semaphore_wait(barrier, len(peers))

    sent = []

    def send(src, dst, device):
        n = len(sent)
        copy = pltpu.make_async_remote_copy(src, dst, ssem.at[n], rsem.at[n], device_id=device, device_id_type=MESH)
        copy.start()
        sent.append(copy)
        return copy

    def wslice(first, count, slot, core):
        return wg.at[
            pl.ds(first, count),
            pl.ds(pl.multiple_of(slot * PIECE, PIECE), PIECE),
            pl.ds(pl.multiple_of(core * HALF, HALF), HALF),
        ]

    def dp_exchange(src_of, buf):
        return [send(src_of((dp + i) % N_DP), buf.at[dp], ((dp + i) % N_DP, fs)) for i in range(1, N_DP)]

    def z_exchange(buf):
        return [send(buf.at[z], buf.at[z], (dp, ((z + i) % 4) * 4 + y)) for i in range(1, 4)]

    def y_exchange(buf):
        return [send(buf.at[y], buf.at[y], (dp, z * 4 + (y + i) % 4)) for i in range(1, 4)]

    def arrive(copies):
        for copy in copies:
            copy.wait_recv()

    def total(buf, n):
        t = buf[0]
        for i in range(1, n):
            t = t + buf[i]
        return t

    def product(f, j, cols=slice(None)):
        return dot_tn(ctx_v[f], cot_v[:, cols]) + dot_tn(ctxp[j], cotp[:, cols])

    exchange = {}

    def send_columns(step):
        j = EXCHANGE_ORDER[step]
        owner = 3 - aA if j < 4 else aA
        exchange[j] = send(ctx_v.at[fid(owner, border[j % 4])], ctxp.at[j], at(aA, b))

    first = {}

    def make_first(k, half):
        if half == 0:
            exchange[k].wait_recv()
        cols = pl.ds(half * HALF, HALF)
        s1s[k, :, cols] = product(fid(aB, border[k]), k, cols).astype(BF16)
        first[k, half] = send(s1s.at[k, :, cols], s1r.at[k, :, cols], at(aB, b))

    def make_second(k):
        exchange[4 + k].wait_recv()
        first[k, 0].wait_recv()
        first[k, 1].wait_recv()
        rsend[k] = (product(fid(a, border[k]), 4 + k) + s1r[k].astype(F32)).astype(BF16)

    low, high = pl.ds(0, 256), pl.ds(256, 256)

    ring = {}

    def group(i):
        return xor2(a, int(mask_of(i)))

    def x_own(i, part):
        src = wslice(group(i) * 4 + part * 2, 2, x, c)
        ring[i, part, "right"] = send(src, src, right_chip)
        ring[i, part, "left"] = send(src, src, left_chip)

    def x_forward(i):
        ring[i, 0, "right"].wait_recv()
        ring[i, 1, "left"].wait_recv()
        src = wslice(group(i) * 4, 2, xL, c)
        ring[i, 2, "right"] = send(src, src, right_chip)
        src = wslice(group(i) * 4 + 2, 2, xR, c)
        ring[i, 2, "left"] = send(src, src, left_chip)

    across = {}

    def x_finish(i):
        ring[i, 0, "left"].wait_recv()
        ring[i, 1, "right"].wait_recv()
        ring[i, 2, "right"].wait_recv()
        ring[i, 2, "left"].wait_recv()
        across[i] = [
            send(wg.at[group(i) * 4 + j, :, my_cols], wg.at[j * 4 + group(i), :, my_cols], sibling) for j in range(4)
        ]

    def multiply(i):
        arrive(across[i])

        def step(t, carry):
            ga = xor2(a, mask_of(jnp.minimum(t, i)))
            gb = xor2(b, mask_of(jnp.minimum(i, 2 * i - t)))

            cols = pl.ds(pl.multiple_of(fid(ga, gb) * CH, CH), CH)
            grad_ref[:, cols] = dot_nt(cot_v[...], wg[ga * 4 + gb]).astype(BF16)
            return carry

        lax.fori_loop(0, 2 * i + 1, step, 0)

    def send_cotangent(half):
        cols = pl.ds(half * HALF, HALF)
        return send(cot_h.at[:, cols], cotp.at[:, cols], at(aA, b))

    cot_low = send_cotangent(0)
    w_load.wait()
    own = wslice(a * 4 + b, 1, x, c)
    w_a = send(own, own, at(a, bA))
    w_b = send(own, own, at(a, bB))
    cot_load.wait()
    seed32 = stack(jnp.concatenate([seed_ref[...], seed_ref[...]], axis=0))
    q32 = stack(fold(dot_nt(seed32, cot_v[...])))
    pltpu.make_async_copy(ctx_v, ctx_v, lsem.at[1]).wait()
    send_columns(0)
    cot_high = send_cotangent(1)
    w_a.wait_recv()
    src = wslice(a * 4 + bA, 1, x, c)
    w_f = send(src, src, at(a, bB))
    w_b.wait_recv()
    w_f.wait_recv()
    src = wslice(a * 4, 4, x, c)
    g_b = send(src, src, at(aB, b))
    x_own(0, 0)
    x_own(0, 1)

    def left_terms(s, carry):
        even = fold(dot_nn(q32, ctx_v[2 * s]))
        odd = fold(dot_nn(q32, ctx_v[2 * s + 1]))
        ppart[s] = jnp.where(row8 < 4, even, odd) * SCALE
        return carry

    lax.fori_loop(0, N_DP, left_terms, 0)
    err_load.wait()
    err_term = fold(dot_nt(seed32, err_v[...]))
    mine8 = (row8 // 4) == (fs % 2)
    ppart[fs // 2] = ppart[fs // 2] + jnp.where(mine8, err_term, 0.0)

    rb1[dp] = ppart[dp]
    ph1 = dp_exchange(lambda peer: ppart.at[peer], rb1)

    send_columns(1)
    cot_low.wait_recv()
    make_first(0, 0)
    cot_high.wait_recv()
    make_first(0, 1)
    arrive(ph1)
    rb2[z] = total(rb1, N_DP)
    ph2 = z_exchange(rb2)
    g_b.wait_recv()
    x_own(1, 0)
    x_forward(0)
    send_columns(2)
    make_first(1, 0)
    arrive(ph2)
    rb3[y] = total(rb2, 4)
    ph3 = y_exchange(rb3)

    send_columns(3)
    make_first(1, 1)
    arrive(ph3)
    pall[dp] = total(rb3, 4)
    ph4 = dp_exchange(lambda peer: pall.at[dp], pall)

    src = wslice(a * 4, 4, x, c)
    g_a = send(src, src, at(aA, b))
    x_own(1, 1)
    make_second(0)
    opp_low = send(rsend.at[0, low], opp.at[0], at(a, bP))
    opp_high = send(rsend.at[0, high], opp.at[1], at(a, bM))
    make_first(2, 0)
    arrive(ph4)

    send_columns(4)
    x_forward(1)

    def inner(u, v):
        t = u[0] * v[0] + u[1] * v[1]
        return jnp.sum(jnp.sum(t, axis=1, keepdims=True), axis=0, keepdims=True)

    basis = []
    for j in range(4):
        v = (pall[:, j, :], pall[:, j + 4, :])
        if j:
            coeffs = [inner(q, v) for q in basis]
            cut0 = coeffs[0] * basis[0][0]
            cut1 = coeffs[0] * basis[0][1]
            for k in range(1, j):
                cut0 = cut0 + coeffs[k] * basis[k][0]
                cut1 = cut1 + coeffs[k] * basis[k][1]
            v = (v[0] - cut0, v[1] - cut1)
        length = jnp.sqrt(inner(v, v) + EPSILON)
        v = (v[0] / length, v[1] / length)
        basis.append(v)
        phat[:, j, :] = v[0]
        phat[:, j + 4, :] = v[1]

    def rows_terms(s, carry):
        p32 = stack(phat[s])
        return carry[0] + dot_nt(p32, ctx_v[2 * s]), carry[1] + dot_nt(p32, ctx_v[2 * s + 1])

    zero = jnp.zeros((32, TOK), F32)
    even, odd = lax.fori_loop(0, N_DP, rows_terms, (zero, zero))
    mix = jnp.where(row8 < 4, fold(even), fold(odd))
    h8 = mix + jnp.concatenate([mix[4:8], mix[0:4]], axis=0)
    slot_rows = phat[fs // 2]
    turned = jnp.concatenate([slot_rows[4:8], slot_rows[0:4]], axis=0)
    p8 = jnp.where(mine8, slot_rows, turned)
    r8 = fold(dot_nn(stack(h8), cot_v[...])) * SCALE + fold(dot_nn(stack(p8), err_v[...]))
    rb5[dp] = jnp.where(row8 < 4, r8[:, 0:512], r8[:, 512:1024])
    ph5 = dp_exchange(lambda peer: rb5.at[dp], rb5)

    make_first(2, 1)
    send_columns(5)
    g_a.wait_recv()
    src = wslice(aA * 4, 4, x, c)
    g_f = send(src, src, at(aB, b))
    x_own(2, 0)
    arrive(ph5)
    rb6[z] = total(rb5, N_DP)
    ph6 = z_exchange(rb6)

    send_columns(6)
    x_own(2, 1)
    make_second(1)
    direct_r = send(rsend.at[1, high], fin.at[0, high], at(a, bP))
    opp_low.wait_recv()
    rsend[1, low] = (rsend[1, low].astype(F32) + opp[0].astype(F32)).astype(BF16)
    through_r = send(rsend.at[1, low], fin.at[0, low], at(a, bP))
    arrive(ph6)
    rb7[y] = total(rb6, 4)
    ph7 = y_exchange(rb7)

    send_columns(7)
    make_first(3, 0)
    make_first(3, 1)
    x_finish(0)
    x_forward(2)
    g_f.wait_recv()
    x_own(3, 0)
    x_own(3, 1)
    arrive(ph7)
    factor = total(rb7, 4) * (1.0 / N_DP)
    right_ref[:, 0:512] = factor[0:4]
    right_ref[:, 512:1024] = factor[4:8]
    ph, pm, plo = parts(p8)
    rh, rm, rl = parts(factor)
    lhs = jnp.concatenate([ph, ph, pm, ph, plo, pm], axis=0).astype(BF16)
    rhs = jnp.concatenate([rh, rm, rh, rl, rh, rm], axis=0)
    row48 = lax.broadcasted_iota(jnp.int32, rhs.shape, 0) % 8
    rhs = jnp.concatenate([jnp.where(row48 < 4, rhs, 0.0), jnp.where(row48 >= 4, rhs, 0.0)], axis=1).astype(BF16)
    base[...] = err_v[...].astype(F32) - dot_tn(lhs, rhs)

    multiply(0)
    make_second(2)
    direct_l = send(rsend.at[2, low], fin.at[1, low], at(a, bM))
    opp_high.wait_recv()
    rsend[2, high] = (rsend[2, high].astype(F32) + opp[1].astype(F32)).astype(BF16)
    through_l = send(rsend.at[2, high], fin.at[1, high], at(a, bM))
    x_finish(1)
    exchange[7].wait_recv()
    base[...] += product(fid(a, b), 7) * SCALE
    multiply(1)
    x_finish(2)
    x_forward(3)
    multiply(2)

    for half, rows, copies in (
        (0, low, (first[3, 0], first[3, 1], through_r, direct_l)),
        (1, high, (direct_r, through_l)),
    ):
        arrive(copies)
        gathered = s1r[3, rows].astype(F32) + (fin[0, rows].astype(F32) + fin[1, rows].astype(F32))
        newmem_ref[rows, :] = (base[rows, :] + gathered * SCALE).astype(BF16)

    x_finish(3)
    multiply(3)
    for copy in sent:
        copy.wait_send()


N_SEMS = 160


def shards(context, cotangent, out_weight, error_memory, seed_factor):
    vmem, hbm = pl.BlockSpec(memory_space=pltpu.VMEM), pl.BlockSpec(memory_space=pl.ANY)
    small = pltpu.VMEM((8, 8, 512), F32)
    quad = pltpu.VMEM((4, 8, 512), F32)
    context_grad, new_memory, right_factor = pl.pallas_call(
        kernel,
        out_shape=(
            pltpu.VMEM((TOK, CH * N_FSDP), BF16),
            pltpu.VMEM((CH, D), BF16),
            pltpu.VMEM((4, D), F32),
        ),
        in_specs=[vmem, hbm, hbm, hbm, hbm],
        out_specs=(vmem, vmem, vmem),
        scratch_shapes=[
            pltpu.VMEM((N_FSDP, TOK, CH), BF16),
            pltpu.VMEM((TOK, D), BF16),
            pltpu.VMEM((CH, D), BF16),
            pltpu.VMEM((TOK, D), BF16),
            pltpu.VMEM((8, TOK, CH), BF16),
            pltpu.VMEM((4, CH, D), BF16),
            pltpu.VMEM((4, CH, D), BF16),
            pltpu.VMEM((3, CH, D), BF16),
            pltpu.VMEM((2, 256, D), BF16),
            pltpu.VMEM((2, CH, D), BF16),
            pltpu.VMEM((N_FSDP, CH, D), BF16),
            pltpu.VMEM((CH, D), F32),
            small, small, quad, quad, small, small, small, quad, quad,
            pltpu.SemaphoreType.DMA((4,)),
            pltpu.SemaphoreType.DMA((N_SEMS,)),
            pltpu.SemaphoreType.DMA((N_SEMS,)),
        ],
        compiler_params=pltpu.CompilerParams(
            collective_id=0, has_side_effects=True, vmem_limit_bytes=52 * 2**20
        ),
        cost_estimate=pl.CostEstimate(flops=18 * 2**30, bytes_accessed=20 * 2**20, transcendentals=0),
        name="projection_gradient",
    )(seed_factor, cotangent, context, out_weight, error_memory[0])
    return context_grad, new_memory[None], right_factor


def solution(mesh):
    placed = (
        P(("dp", "fsdp"), None),
        P(("dp", "fsdp"), None),
        P("fsdp", None),
        P("dp", "fsdp", None),
        P(),
    )
    return jax.shard_map(
        shards,
        mesh=mesh,
        in_specs=placed,
        out_specs=(P(("dp", "fsdp"), None), P("dp", "fsdp", None), P()),
        check_vma=False,
    )
```

```python
import functools

import jax
import jax.numpy as jnp
import numpy as np
from jax import lax
from jax.experimental import pallas as pl
from jax.experimental.pallas import tpu as pltpu
from jax.sharding import PartitionSpec as P

MESH = pl.DeviceIdType.MESH
F32 = jnp.float32
BF16 = jnp.bfloat16
EPSILON = 1e-06
TOK = 512
CH = 512
D = 1024
N_DP = 8
N_FSDP = 16
PIECE = 128
HALF = 512
SCALE = float(np.float32(1.0) / np.sqrt(np.float32(TOK * N_FSDP)))
ORDER = (
    "w0", "E0", "q", "cot1", "P0", "wf", "xa", "P1", "ph1", "gb", "cot0", "x01", "m00", "ph2", "ga",
    "F01", "x10", "x11", "f0", "E4", "F00", "ph3", "ph4", "E2", "gf", "x20", "x21", "E1", "S0",
    "sb0", "f1", "GS", "h0", "F20", "F21", "E5", "h1", "h2", "ph5", "f2", "E3", "x30", "F10", "x31",
    "sb1", "m10", "F11", "E6", "m01", "ph6", "m11", "m21", "sb2", "m20", "ph7", "F30", "F31", "E7",
    "m02", "m12", "m22", "S2", "f3", "S1", "base0", "base1", "tl", "b70", "b71", "sb3", "tr", "m30",
    "m31", "m32", "m03", "m13", "m23", "m33", "fin0", "fin1",
)


def dot_tn(a, b):
    return lax.dot_general(a, b, (((0,), (0,)), ((), ())), preferred_element_type=F32)


def dot_nn(a, b):
    return lax.dot_general(a, b, (((1,), (0,)), ((), ())), preferred_element_type=F32)


def dot_nt(a, b):
    return lax.dot_general(a, b, (((1,), (1,)), ((), ())), preferred_element_type=F32)


def parts(v):
    hi = v.astype(BF16).astype(F32)
    rest = v - hi
    mid = rest.astype(BF16).astype(F32)
    return hi, mid, rest - mid


def stack(v):
    hi, mid, lo = parts(v)
    return jnp.concatenate([hi, mid, lo, jnp.zeros_like(hi)], axis=0).astype(BF16)


def fold(r):
    return r[0:8] + (r[8:16] + r[16:24])


def xor2(a, m):
    return ((a // 2 + m // 2) % 2) * 2 + (a % 2 + m % 2) % 2


def mask_of(i):
    return ((i + 1) % 3 + 1) * ((i + 2) // 3)


def kernel(
    seed_ref, cot_h, ctx_h, w_h, err_h,
    grad_ref, newmem_ref, right_ref,
    ctx_v, cot_v, err_v, cotp, ctxp, s1s, s1r, rsend, opp, fin, wg, base,
    ppart, rb1, rb2, rb3, pall, phat, rb5, rb6, rb7, hacc, p_own,
    lsem, ssem, rsem,
):
    dp, fs = lax.axis_index("dp"), lax.axis_index("fsdp")
    x, c = dp // 2, dp % 2
    z, y = fs // 4, fs % 4
    a, b = z * (1 - c) + y * c, y * (1 - c) + z * c

    def fid(i, j):
        return (i * (1 - c) + j * c) * 4 + j * (1 - c) + i * c

    def at(i, j):
        return (dp, fid(i, j))

    ga = [a, 3 - a, xor2(a, 1), xor2(a, 2)]
    gb = [b, 3 - b, xor2(b, 1), xor2(b, 2)]
    aB, aA, bB, bA = ga[1], ga[2], gb[1], gb[2]
    bP, bM = (b + 1) % 4, (b + 3) % 4
    xR, xL = (x + 1) % 4, (x + 3) % 4
    right_chip, left_chip = (xR * 2 + c, fs), (xL * 2 + c, fs)
    sibling = (x * 2 + 1 - c, fs)
    border = [(b + k) % 4 for k in (2, 1, 3, 0)]
    row8 = lax.broadcasted_iota(jnp.int32, (8, CH), 0)
    mine8 = (row8 // 4) == (fs % 2)
    low, high = pl.ds(0, 256), pl.ds(256, 256)
    halves = (pl.ds(0, HALF), pl.ds(HALF, HALF))

    loads = {}

    def load(name, src, dst):
        loads[name] = pltpu.make_async_copy(src, dst, lsem.at[len(loads)])
        loads[name].start()

    load("cot", cot_h, cot_v)
    load("w", w_h, wg.at[a * 4 + b])
    for f in range(N_FSDP):
        pltpu.make_async_copy(ctx_h.at[:, pl.ds(f * CH, CH)], ctx_v.at[f], lsem.at[3]).start()
    load("err", err_h, err_v)
    loads["ctx"] = pltpu.make_async_copy(ctx_v, ctx_v, lsem.at[3])

    barrier = pltpu.get_barrier_semaphore()
    peers = [((dp + i) % N_DP, fs) for i in range(1, N_DP)]
    peers += [at((a + i) % 4, b) for i in range(1, 4)]
    peers += [at(a, (b + i) % 4) for i in range(1, 4)]
    for peer in peers:
        pl.semaphore_signal(barrier, inc=1, device_id=peer, device_id_type=MESH)
    pl.semaphore_wait(barrier, len(peers))

    sent, flights, arrived = [], {}, set()

    def send(name, src, dst, device):
        n = len(sent)
        copy = pltpu.make_async_remote_copy(src, dst, ssem.at[n], rsem.at[n], device_id=device, device_id_type=MESH)
        copy.start()
        sent.append(copy)
        flights.setdefault(name, []).append(copy)

    def need(*names):
        for name in names:
            if name in loads:
                loads.pop(name).wait()
            elif name in flights and name not in arrived:
                arrived.add(name)
                for copy in flights[name]:
                    copy.wait_recv()
            else:
                assert name in arrived or name in ("cot", "w", "err", "ctx"), name

    def dp_exchange(name, src_of, buf):
        for i in range(1, N_DP):
            send(name, src_of((dp + i) % N_DP), buf.at[dp], ((dp + i) % N_DP, fs))

    def a_exchange(name, buf):
        for i in range(1, 4):
            send(name, buf.at[a], buf.at[a], at((a + i) % 4, b))

    def b_exchange(name, buf):
        for i in range(1, 4):
            send(name, buf.at[b], buf.at[b], at(a, (b + i) % 4))

    def total(buf, n):
        t = buf[0]
        for i in range(1, n):
            t = t + buf[i]
        return t

    def task_q():
        need("cot")
        seed32 = stack(jnp.concatenate([seed_ref[...], seed_ref[...]], axis=0))
        hacc[0] = dot_nt(seed32, cot_v[...])
        need("err")
        p_own[...] = jnp.where(mine8, fold(dot_nt(seed32, err_v[...])), 0.0)

    def left_terms(first, last):
        need("ctx")
        q32 = stack(fold(hacc[0]))

        def step(s, carry):
            even = fold(dot_nn(q32, ctx_v[2 * s]))
            odd = fold(dot_nn(q32, ctx_v[2 * s + 1]))
            ppart[s] = jnp.where(row8 < 4, even, odd) * SCALE
            return carry

        lax.fori_loop(first, last, step, 0)

    def task_P1():
        left_terms(4, 8)
        ppart[fs // 2] = ppart[fs // 2] + p_own[...]
        rb1[dp] = ppart[dp]

    def task_ph2():
        need("ph1")
        rb2[a] = total(rb1, N_DP)
        a_exchange("ph2", rb2)

    def task_ph3():
        need("ph2")
        rb3[b] = total(rb2, 4)
        b_exchange("ph3", rb3)

    def task_ph4():
        need("ph3")
        pall[dp] = total(rb3, 4)
        dp_exchange("ph4", lambda peer: pall.at[dp], pall)

    def inner(u, v):
        t = u[0] * v[0] + u[1] * v[1]
        return jnp.sum(jnp.sum(t, axis=1, keepdims=True), axis=0, keepdims=True)

    def task_GS():
        need("ph4")
        basis = []
        for j in range(4):
            v = (pall[:, j, :], pall[:, j + 4, :])
            if j:
                coeffs = [inner(q, v) for q in basis]
                cut0 = coeffs[0] * basis[0][0]
                cut1 = coeffs[0] * basis[0][1]
                for k in range(1, j):
                    cut0 = cut0 + coeffs[k] * basis[k][0]
                    cut1 = cut1 + coeffs[k] * basis[k][1]
                v = (v[0] - cut0, v[1] - cut1)
            length = jnp.sqrt(inner(v, v) + EPSILON)
            v = (v[0] / length, v[1] / length)
            basis.append(v)
            phat[:, j, :] = v[0]
            phat[:, j + 4, :] = v[1]

    def rows_terms(first, last):
        def step(s, carry):
            p32 = stack(phat[s])
            return carry[0] + dot_nt(p32, ctx_v[2 * s]), carry[1] + dot_nt(p32, ctx_v[2 * s + 1])

        return lax.fori_loop(first, last, step, (hacc[0], hacc[1]))

    def task_h0():
        hacc[...] = jnp.zeros_like(hacc)
        hacc[0], hacc[1] = rows_terms(0, 4)

    def task_h1():
        hacc[0], hacc[1] = rows_terms(4, 8)

    def task_h2():
        mix = jnp.where(row8 < 4, fold(hacc[0]), fold(hacc[1]))
        h8 = mix + jnp.concatenate([mix[4:8], mix[0:4]], axis=0)
        slot_rows = phat[fs // 2]
        turned = jnp.concatenate([slot_rows[4:8], slot_rows[0:4]], axis=0)
        p8 = jnp.where(mine8, slot_rows, turned)
        p_own[...] = p8
        r8 = fold(dot_nn(stack(h8), cot_v[...])) * SCALE + fold(dot_nn(stack(p8), err_v[...]))
        rb5[a] = jnp.where(row8 < 4, r8[:, 0:512], r8[:, 512:1024])

    def task_ph6():
        need("ph5")
        rb6[b] = total(rb5, 4)
        b_exchange("ph6", rb6)

    def task_ph7():
        need("ph6")
        rb7[dp] = total(rb6, 4)
        dp_exchange("ph7", lambda peer: rb7.at[dp], rb7)

    def approx(half, factor):
        ph, pm, plo = parts(p_own[...])
        rh, rm, rl = parts(jnp.where((row8 // 4) == half, factor, 0.0))
        lhs = jnp.concatenate([ph, ph, pm, ph, plo, pm], axis=0).astype(BF16)
        rhs = jnp.concatenate([rh, rm, rh, rl, rh, rm], axis=0).astype(BF16)
        base[:, halves[half]] = err_v[:, halves[half]].astype(F32) - dot_tn(lhs, rhs)

    def task_base0():
        need("ph7")
        factor = total(rb7, N_DP) * (1.0 / N_DP)
        hacc[0, 0:8] = factor
        right_ref[:, 0:512] = factor[0:4]
        right_ref[:, 512:1024] = factor[4:8]
        approx(0, factor)

    def task_cot(half):
        cols = halves[half]
        send(f"cot{half}", cot_h.at[:, cols], cotp.at[:, cols], at(aA, b))

    def task_E(j):
        need("ctx")
        send(f"E{j}", ctx_v.at[fid(3 - aA if j < 4 else aA, border[j % 4])], ctxp.at[j], at(aA, b))

    def product(f, j, cols=slice(None)):
        return dot_tn(ctx_v[f], cot_v[:, cols]) + dot_tn(ctxp[j], cotp[:, cols])

    def task_F(k, half):
        need("cot", f"E{k}", f"cot{half}")
        cols = halves[half]
        s1s[k, :, cols] = product(fid(aB, border[k]), k, cols).astype(BF16)
        send(f"F{k}{half}", s1s.at[k, :, cols], s1r.at[k, :, cols], at(aB, b))

    def task_S(k):
        need(f"E{4 + k}", f"F{k}0", f"F{k}1", "cot0", "cot1")
        rsend[k] = (product(fid(a, border[k]), 4 + k) + s1r[k].astype(F32)).astype(BF16)
        if k == 0:
            send("ol", rsend.at[0, low], opp.at[0], at(a, bP))
            send("oh", rsend.at[0, high], opp.at[1], at(a, bM))
        elif k == 1:
            send("dr", rsend.at[1, high], fin.at[0, high], at(a, bP))
        else:
            send("dl", rsend.at[2, low], fin.at[1, low], at(a, bM))

    def task_tr():
        need("ol")
        rsend[1, low] = (rsend[1, low].astype(F32) + opp[0].astype(F32)).astype(BF16)
        send("tr", rsend.at[1, low], fin.at[0, low], at(a, bP))

    def task_tl():
        need("oh")
        rsend[2, high] = (rsend[2, high].astype(F32) + opp[1].astype(F32)).astype(BF16)
        send("tl", rsend.at[2, high], fin.at[1, high], at(a, bM))

    def task_b7(half):
        need("E7", "cot0", "cot1")
        base[:, halves[half]] += product(fid(a, b), 7, halves[half]) * SCALE

    def task_fin(half):
        need("F30", "F31", *(("tr", "dl") if half == 0 else ("dr", "tl")))
        rows = (low, high)[half]
        gathered = s1r[3, rows].astype(F32) + (fin[0, rows].astype(F32) + fin[1, rows].astype(F32))
        newmem_ref[rows, :] = (base[rows, :] + gathered * SCALE).astype(BF16)

    def wslice(first, count, slot, rows=PIECE, shift=0):
        return wg.at[
            pl.ds(first, count),
            pl.ds(pl.multiple_of(slot * PIECE + shift, rows), rows),
            pl.ds(pl.multiple_of(c * HALF, HALF), HALF),
        ]

    def pass_on(name, src, device):
        send(name, src, src, device)

    def task_w0():
        need("w")
        pass_on("wa", wslice(a * 4 + b, 1, x), at(a, bA))
        pass_on("wb", wslice(a * 4 + b, 1, x), at(a, bB))

    def task_wf():
        need("wa")
        pass_on("wf", wslice(a * 4 + bA, 1, x), at(a, bB))

    def task_group(name, needed, source, target):
        need(*needed)
        pass_on(name, wslice(source * 4, 4, x), at(target, b))

    def both(name, first, count):
        pass_on(name + "r", wslice(first, count, x), right_chip)
        pass_on(name + "l", wslice(first, count, x), left_chip)

    def task_xa():
        need("wa")
        both("xa", a * 4 + bA, 1)

    other_pair = a * 4 + (1 - b // 2) * 2

    def task_x01():
        need("wb", "wf")
        both("x01", other_pair, 2)

    def task_x(i, part):
        need((None, "gb", "ga", "gf")[i])
        both(f"x{i}{part}", ga[i] * 4 + part * 2, 2)

    def task_f(i):
        if i == 0:
            need("xar", "xal", "x01r", "x01l")
            pass_on("f0", wslice(a * 4 + bA, 1, xL, 64, 0), right_chip)
            pass_on("f0", wslice(a * 4 + bA, 1, xR, 64, 64), left_chip)
            pass_on("f0", wslice(other_pair, 1, xL), right_chip)
            pass_on("f0", wslice(other_pair + 1, 1, xR), left_chip)
        else:
            need(f"x{i}0r", f"x{i}1l")
            pass_on(f"f{i}", wslice(ga[i] * 4, 2, xL), right_chip)
            pass_on(f"f{i}", wslice(ga[i] * 4 + 2, 2, xR), left_chip)

    def ring_done(i):
        if i:
            need(f"x{i}0r", f"x{i}1l", f"x{i}0l", f"x{i}1r", f"f{i}")
        else:
            need("xar", "xal", "x01r", "x01l", "f0")

    def task_sb(i):
        ring_done(i)
        cols = pl.ds(pl.multiple_of(c * HALF, HALF), HALF)
        for u in range(4):
            if i + u:
                send(f"sb{i}{u}", wg.at[ga[i] * 4 + gb[u], :, cols], wg.at[gb[u] * 4 + ga[i], :, cols], sibling)

    def task_m(i, u):
        need("cot")
        if i + u:
            ring_done(i)
            need(f"sb{u}{i}")
        else:
            need("w")
        cols = pl.ds(pl.multiple_of(fid(ga[i], gb[u]) * CH, CH), CH)
        grad_ref[:, cols] = dot_nt(cot_v[...], wg[ga[i] * 4 + gb[u]]).astype(BF16)

    tasks = {
        "w0": task_w0, "wf": task_wf, "xa": task_xa, "x01": task_x01,
        "gb": functools.partial(task_group, "gb", ("wa", "wb", "wf"), a, aB),
        "ga": functools.partial(task_group, "ga", ("wa", "wb", "wf"), a, aA),
        "gf": functools.partial(task_group, "gf", ("ga",), aA, aB),
        "q": task_q, "P0": functools.partial(left_terms, 0, 4), "P1": task_P1,
        "ph1": functools.partial(dp_exchange, "ph1", lambda peer: ppart.at[peer], rb1),
        "ph2": task_ph2, "ph3": task_ph3, "ph4": task_ph4,
        "GS": task_GS, "h0": task_h0, "h1": task_h1, "h2": task_h2,
        "ph5": functools.partial(a_exchange, "ph5", rb5), "ph6": task_ph6, "ph7": task_ph7,
        "base0": task_base0, "base1": lambda: approx(1, hacc[0, 0:8]),
        "tr": task_tr, "tl": task_tl,
    }
    for i in range(8):
        tasks[f"E{i}"] = functools.partial(task_E, i)
    for i in range(4):
        tasks[f"f{i}"] = functools.partial(task_f, i)
        tasks[f"sb{i}"] = functools.partial(task_sb, i)
        if i < 3:
            tasks[f"S{i}"] = functools.partial(task_S, i)
        for u in range(4):
            tasks[f"m{i}{u}"] = functools.partial(task_m, i, u)
        for u in range(2):
            tasks[f"F{i}{u}"] = functools.partial(task_F, i, u)
            if i:
                tasks[f"x{i}{u}"] = functools.partial(task_x, i, u)
    for u in range(2):
        tasks[f"cot{u}"] = functools.partial(task_cot, u)
        tasks[f"b7{u}"] = functools.partial(task_b7, u)
        tasks[f"fin{u}"] = functools.partial(task_fin, u)

    assert sorted(ORDER) == sorted(tasks)
    for name in ORDER:
        tasks[name]()

    need(*(name for name in flights))
    for copy in sent:
        copy.wait_send()


N_SEMS = 160


def shards(context, cotangent, out_weight, error_memory, seed_factor):
    vmem, hbm = pl.BlockSpec(memory_space=pltpu.VMEM), pl.BlockSpec(memory_space=pl.ANY)
    small = pltpu.VMEM((8, 8, 512), F32)
    quad = pltpu.VMEM((4, 8, 512), F32)
    context_grad, new_memory, right_factor = pl.pallas_call(
        kernel,
        out_shape=(
            pltpu.VMEM((TOK, CH * N_FSDP), BF16),
            pltpu.VMEM((CH, D), BF16),
            pltpu.VMEM((4, D), F32),
        ),
        in_specs=[vmem, hbm, hbm, hbm, hbm],
        out_specs=(vmem, vmem, vmem),
        scratch_shapes=[
            pltpu.VMEM((N_FSDP, TOK, CH), BF16),
            pltpu.VMEM((TOK, D), BF16),
            pltpu.VMEM((CH, D), BF16),
            pltpu.VMEM((TOK, D), BF16),
            pltpu.VMEM((8, TOK, CH), BF16),
            pltpu.VMEM((4, CH, D), BF16),
            pltpu.VMEM((4, CH, D), BF16),
            pltpu.VMEM((3, CH, D), BF16),
            pltpu.VMEM((2, 256, D), BF16),
            pltpu.VMEM((2, CH, D), BF16),
            pltpu.VMEM((N_FSDP, CH, D), BF16),
            pltpu.VMEM((CH, D), F32),
            small, small, quad, quad, small, small, quad, quad, small,
            pltpu.VMEM((2, 32, TOK), F32),
            pltpu.VMEM((8, CH), F32),
            pltpu.SemaphoreType.DMA((4,)),
            pltpu.SemaphoreType.DMA((N_SEMS,)),
            pltpu.SemaphoreType.DMA((N_SEMS,)),
        ],
        compiler_params=pltpu.CompilerParams(
            collective_id=0, has_side_effects=True, vmem_limit_bytes=52 * 2**20
        ),
        cost_estimate=pl.CostEstimate(flops=18 * 2**30, bytes_accessed=20 * 2**20, transcendentals=0),
        name="projection_gradient",
    )(seed_factor, cotangent, context, out_weight, error_memory[0])
    return context_grad, new_memory[None], right_factor


def solution(mesh):
    placed = (
        P(("dp", "fsdp"), None),
        P(("dp", "fsdp"), None),
        P("fsdp", None),
        P("dp", "fsdp", None),
        P(),
    )
    return jax.shard_map(
        shards,
        mesh=mesh,
        in_specs=placed,
        out_specs=(P(("dp", "fsdp"), None), P("dp", "fsdp", None), P()),
        check_vma=False,
    )
```

```python
import functools

import jax
import jax.numpy as jnp
import numpy as np
from jax import lax
from jax.experimental import pallas as pl
from jax.experimental.pallas import tpu as pltpu
from jax.sharding import PartitionSpec as P

MESH = pl.DeviceIdType.MESH
F32 = jnp.float32
BF16 = jnp.bfloat16
EPSILON = 1e-06
TOK = 512
CH = 512
D = 1024
N_DP = 8
N_FSDP = 16
PIECE = 128
HALF = 512
SCALE = float(np.float32(1.0) / np.sqrt(np.float32(TOK * N_FSDP)))
CUT = 256
ORDER = (
    "w0", "q", "E1", "cot1", "gB0", "P0", "E0b", "xa", "wf", "P1", "ph1", "gB1", "x01", "gB2",
    "m00", "ph2", "E0", "ga", "cot0", "x10", "F11", "x11", "ph3", "F01", "ph4", "cot0b", "gf",
    "x20", "E2", "x21", "F00", "GS", "E4", "f1", "F10", "h0", "F00b", "f0", "h1", "h2", "F00c",
    "f2", "ph5", "E3", "E6", "F21", "sb1", "S0", "F30", "x30", "sb0", "E5", "ph6", "m01", "F20",
    "m11", "x31", "sb2", "F31", "E7", "m20", "m10", "m12", "m22", "m02", "m21", "ph7", "f3", "S1",
    "tA", "S2", "tB", "base0", "base1", "sb3", "m31", "m32", "b70", "m30", "m13", "b71", "m23",
    "m33", "fin0", "m03", "fin1",
)


def dot_tn(a, b):
    return lax.dot_general(a, b, (((0,), (0,)), ((), ())), preferred_element_type=F32)


def dot_nn(a, b):
    return lax.dot_general(a, b, (((1,), (0,)), ((), ())), preferred_element_type=F32)


def dot_nt(a, b):
    return lax.dot_general(a, b, (((1,), (1,)), ((), ())), preferred_element_type=F32)


def parts(v):
    hi = v.astype(BF16).astype(F32)
    rest = v - hi
    mid = rest.astype(BF16).astype(F32)
    return hi, mid, rest - mid


def stack(v):
    hi, mid, lo = parts(v)
    return jnp.concatenate([hi, mid, lo, jnp.zeros_like(hi)], axis=0).astype(BF16)


def fold(r):
    return r[0:8] + (r[8:16] + r[16:24])


def xor2(a, m):
    return ((a // 2 + m // 2) % 2) * 2 + (a % 2 + m % 2) % 2


def mask_of(i):
    return ((i + 1) % 3 + 1) * ((i + 2) // 3)


def kernel(
    seed_ref, cot_h, ctx_h, w_h, err_h,
    grad_ref, newmem_ref, right_ref,
    ctx_v, cot_v, err_v, cotp, ctxp, s1s, s1r, rsend, opp, fin, wg, base,
    ppart, rb1, rb2, rb3, pall, phat, rb5, rb6, rb7, hacc, p_own,
    lsem, ssem, rsem,
):
    dp, fs = lax.axis_index("dp"), lax.axis_index("fsdp")
    x, c = dp // 2, dp % 2
    z, y = fs // 4, fs % 4
    a, b = z * (1 - c) + y * c, y * (1 - c) + z * c

    def fid(i, j):
        return (i * (1 - c) + j * c) * 4 + j * (1 - c) + i * c

    def at(i, j):
        return (dp, fid(i, j))

    ga = [a, 3 - a, xor2(a, 1), xor2(a, 2)]
    gb = [b, 3 - b, xor2(b, 1), xor2(b, 2)]
    aB, aA, bB, bA = ga[1], ga[2], gb[1], gb[2]
    xR, xL = (x + 1) % 4, (x + 3) % 4
    right_chip, left_chip = (xR * 2 + c, fs), (xL * 2 + c, fs)
    sibling = (x * 2 + 1 - c, fs)
    border = [gb[3], bA, bB, b]
    row8 = lax.broadcasted_iota(jnp.int32, (8, CH), 0)
    mine8 = (row8 // 4) == (fs % 2)
    low, high = pl.ds(0, CUT), pl.ds(CUT, CH - CUT)
    halves = (pl.ds(0, HALF), pl.ds(HALF, HALF))

    barrier = pltpu.get_barrier_semaphore()
    peers = [((dp + i) % N_DP, fs) for i in range(1, N_DP)]
    peers += [at((a + i) % 4, b) for i in range(1, 4)]
    peers += [at(a, (b + i) % 4) for i in range(1, 4)]
    for peer in peers:
        pl.semaphore_signal(barrier, inc=1, device_id=peer, device_id_type=MESH)
    loads = {}

    def load(name, src, dst):
        loads[name] = pltpu.make_async_copy(src, dst, lsem.at[len(loads)])
        loads[name].start()

    load("cot", cot_h, cot_v)
    load("w", w_h, wg.at[a * 4 + b])
    for f in range(N_FSDP):
        pltpu.make_async_copy(ctx_h.at[:, pl.ds(f * CH, CH)], ctx_v.at[f], lsem.at[3]).start()
    load("err", err_h, err_v)
    loads["ctx"] = pltpu.make_async_copy(ctx_v, ctx_v, lsem.at[3])

    pl.semaphore_wait(barrier, len(peers))

    sent, flights, arrived = [], {}, set()

    def send(name, src, dst, device):
        n = len(sent)
        copy = pltpu.make_async_remote_copy(src, dst, ssem.at[n], rsem.at[n], device_id=device, device_id_type=MESH)
        copy.start()
        sent.append(copy)
        flights.setdefault(name, []).append(copy)

    def need(*names):
        for name in names:
            if name in loads:
                loads.pop(name).wait()
            elif name in flights and name not in arrived:
                arrived.add(name)
                for copy in flights[name]:
                    copy.wait_recv()
            else:
                assert name in arrived or name in ("cot", "w", "err", "ctx"), name

    def dp_exchange(name, src_of, buf):
        for i in range(1, N_DP):
            send(name, src_of((dp + i) % N_DP), buf.at[dp], ((dp + i) % N_DP, fs))

    def a_exchange(name, buf):
        for i in range(1, 4):
            send(name, buf.at[a], buf.at[a], at((a + i) % 4, b))

    def b_exchange(name, buf):
        for i in range(1, 4):
            send(name, buf.at[b], buf.at[b], at(a, (b + i) % 4))

    def total(buf, n):
        t = buf[0]
        for i in range(1, n):
            t = t + buf[i]
        return t

    def task_q():
        need("cot")
        seed32 = stack(jnp.concatenate([seed_ref[...], seed_ref[...]], axis=0))
        hacc[0] = dot_nt(seed32, cot_v[...])
        need("err")
        p_own[...] = jnp.where(mine8, fold(dot_nt(seed32, err_v[...])), 0.0)

    def left_terms(first, last):
        need("ctx")
        q32 = stack(fold(hacc[0]))

        def step(s, carry):
            even = fold(dot_nn(q32, ctx_v[2 * s]))
            odd = fold(dot_nn(q32, ctx_v[2 * s + 1]))
            ppart[s] = jnp.where(row8 < 4, even, odd) * SCALE
            return carry

        lax.fori_loop(first, last, step, 0)

    def task_P1():
        left_terms(4, 8)
        ppart[fs // 2] = ppart[fs // 2] + p_own[...]
        rb1[dp] = ppart[dp]

    def task_ph2():
        need("ph1")
        rb2[a] = total(rb1, N_DP)
        a_exchange("ph2", rb2)

    def task_ph3():
        need("ph2")
        rb3[b] = total(rb2, 4)
        b_exchange("ph3", rb3)

    def task_ph4():
        need("ph3")
        pall[dp] = total(rb3, 4)
        dp_exchange("ph4", lambda peer: pall.at[dp], pall)

    def inner(u, v):
        t = u[0] * v[0] + u[1] * v[1]
        return jnp.sum(jnp.sum(t, axis=1, keepdims=True), axis=0, keepdims=True)

    def task_GS():
        need("ph4")
        basis = []
        for j in range(4):
            v = (pall[:, j, :], pall[:, j + 4, :])
            if j:
                coeffs = [inner(q, v) for q in basis]
                cut0 = coeffs[0] * basis[0][0]
                cut1 = coeffs[0] * basis[0][1]
                for k in range(1, j):
                    cut0 = cut0 + coeffs[k] * basis[k][0]
                    cut1 = cut1 + coeffs[k] * basis[k][1]
                v = (v[0] - cut0, v[1] - cut1)
            length = jnp.sqrt(inner(v, v) + EPSILON)
            v = (v[0] / length, v[1] / length)
            basis.append(v)
            phat[:, j, :] = v[0]
            phat[:, j + 4, :] = v[1]

    def rows_terms(first, last):
        def step(s, carry):
            p32 = stack(phat[s])
            return carry[0] + dot_nt(p32, ctx_v[2 * s]), carry[1] + dot_nt(p32, ctx_v[2 * s + 1])

        return lax.fori_loop(first, last, step, (hacc[0], hacc[1]))

    def task_h0():
        hacc[...] = jnp.zeros_like(hacc)
        hacc[0], hacc[1] = rows_terms(0, 4)

    def task_h1():
        hacc[0], hacc[1] = rows_terms(4, 8)

    def task_h2():
        mix = jnp.where(row8 < 4, fold(hacc[0]), fold(hacc[1]))
        h8 = mix + jnp.concatenate([mix[4:8], mix[0:4]], axis=0)
        slot_rows = phat[fs // 2]
        turned = jnp.concatenate([slot_rows[4:8], slot_rows[0:4]], axis=0)
        p8 = jnp.where(mine8, slot_rows, turned)
        p_own[...] = p8
        r8 = fold(dot_nn(stack(h8), cot_v[...])) * SCALE + fold(dot_nn(stack(p8), err_v[...]))
        rb5[a] = jnp.where(row8 < 4, r8[:, 0:512], r8[:, 512:1024])

    def task_ph6():
        need("ph5")
        rb6[b] = total(rb5, 4)
        b_exchange("ph6", rb6)

    def task_ph7():
        need("ph6")
        rb7[dp] = total(rb6, 4)
        dp_exchange("ph7", lambda peer: rb7.at[dp], rb7)

    def approx(half, factor):
        ph, pm, plo = parts(p_own[...])
        rh, rm, rl = parts(jnp.where((row8 // 4) == half, factor, 0.0))
        lhs = jnp.concatenate([ph, ph, pm, ph, plo, pm], axis=0).astype(BF16)
        rhs = jnp.concatenate([rh, rm, rh, rl, rh, rm], axis=0).astype(BF16)
        base[:, halves[half]] = err_v[:, halves[half]].astype(F32) - dot_tn(lhs, rhs)

    def task_base0():
        need("ph7")
        factor = total(rb7, N_DP) * (1.0 / N_DP)
        hacc[0, 0:8] = factor
        right_ref[:, 0:512] = factor[0:4]
        right_ref[:, 512:1024] = factor[4:8]
        approx(0, factor)

    def task_cot(name, first, count):
        cols = pl.ds(first, count)
        send(name, cot_h.at[:, cols], cotp.at[:, cols], at(aA, b))

    quarters = (pl.ds(0, 256), pl.ds(256, 256))

    def task_E(j):
        need("ctx")
        send(f"E{j}", ctx_v.at[fid(3 - aA if j < 4 else aA, border[j % 4])], ctxp.at[j], at(aA, b))

    def task_E0(part):
        need("ctx")
        cols = quarters[part]
        send(("E0", "E0b")[part], ctx_v.at[fid(3 - aA, border[0]), :, cols], ctxp.at[0, :, cols], at(aA, b))

    def product(f, j, cols=slice(None), rows=slice(None)):
        return dot_tn(ctx_v[f, :, rows], cot_v[:, cols]) + dot_tn(ctxp[j, :, rows], cotp[:, cols])

    def task_F(k, half):
        need("cot", f"E{k}", *(("cot0", "cot0b") if half == 0 else ("cot1",)))
        if k == 0:
            need("E0b")
        cols = halves[half]
        s1s[k, :, cols] = product(fid(aB, border[k]), k, cols).astype(BF16)
        send(f"F{k}{half}", s1s.at[k, :, cols], s1r.at[k, :, cols], at(aB, b))

    def task_F0(name, needed, rows, cols):
        need("cot", "cot0", *needed)
        s1s[0, rows, cols] = product(fid(aB, border[0]), 0, cols, rows).astype(BF16)
        send(name, s1s.at[0, rows, cols], s1r.at[0, rows, cols], at(aB, b))

    def task_S(k):
        need(f"E{4 + k}", f"F{k}0", f"F{k}1", "cot0", "cot0b", "cot1")
        if k == 0:
            need("F00b", "F00c")
        rsend[k] = (product(fid(a, border[k]), 4 + k) + s1r[k].astype(F32)).astype(BF16)
        if k == 0:
            send("oB", rsend.at[0, low], opp.at[0], at(a, bB))
            send("oA", rsend.at[0, high], opp.at[1, pl.ds(0, CH - CUT)], at(a, bA))
        elif k == 1:
            send("dA", rsend.at[1, high], fin.at[0, high], at(a, bA))
        else:
            send("dB", rsend.at[2, low], fin.at[1, low], at(a, bB))

    def task_tA():
        need("oB")
        rsend[1, low] = (rsend[1, low].astype(F32) + opp[0].astype(F32)).astype(BF16)
        send("tA", rsend.at[1, low], fin.at[0, low], at(a, bA))

    def task_tB():
        need("oA")
        rsend[2, high] = (rsend[2, high].astype(F32) + opp[1, 0:CH - CUT].astype(F32)).astype(BF16)
        send("tB", rsend.at[2, high], fin.at[1, high], at(a, bB))

    def task_b7(half):
        need("E7", "cot0", "cot0b", "cot1")
        base[:, halves[half]] += product(fid(a, b), 7, halves[half]) * SCALE

    def task_fin(half):
        need("F30", "F31", *(("tA", "dB") if half == 0 else ("dA", "tB")))
        rows = (low, high)[half]
        gathered = s1r[3, rows].astype(F32) + (fin[0, rows].astype(F32) + fin[1, rows].astype(F32))
        newmem_ref[rows, :] = (base[rows, :] + gathered * SCALE).astype(BF16)

    def wslice(first, count, slot, rows=PIECE, shift=0):
        return wg.at[
            pl.ds(first, count),
            pl.ds(pl.multiple_of(slot * PIECE + shift, rows), rows),
            pl.ds(pl.multiple_of(c * HALF, HALF), HALF),
        ]

    def pass_on(name, src, device):
        send(name, src, src, device)

    def task_w0():
        need("w")
        pass_on("wa", wslice(a * 4 + b, 1, x), at(a, bA))
        pass_on("wb", wslice(a * 4 + b, 1, x), at(a, bB))

    def task_wf():
        need("wa")
        pass_on("wf", wslice(a * 4 + bA, 1, x), at(a, bB))

    def task_group(name, needed, source, target):
        need(*needed)
        pass_on(name, wslice(source * 4, 4, x), at(target, b))

    def task_block(name, needed, first, count, target):
        need(*needed)
        pass_on(name, wslice(first, count, x), at(target, b))

    def both(name, first, count):
        pass_on(name + "r", wslice(first, count, x), right_chip)
        pass_on(name + "l", wslice(first, count, x), left_chip)

    def task_xa():
        need("wa")
        both("xa", a * 4 + bA, 1)

    other_pair = a * 4 + (1 - b // 2) * 2

    def task_x01():
        need("wb", "wf")
        both("x01", other_pair, 2)

    def task_x(i, part):
        need(*((), ("gB0", "gB1", "gB2"), ("ga",), ("gf",))[i])
        both(f"x{i}{part}", ga[i] * 4 + part * 2, 2)

    def task_f(i):
        if i == 0:
            need("xar", "xal", "x01r", "x01l")
            pass_on("f0", wslice(a * 4 + bA, 1, xL, 64, 0), right_chip)
            pass_on("f0", wslice(a * 4 + bA, 1, xR, 64, 64), left_chip)
            pass_on("f0", wslice(other_pair, 1, xL), right_chip)
            pass_on("f0", wslice(other_pair + 1, 1, xR), left_chip)
        else:
            need(f"x{i}0r", f"x{i}1l")
            pass_on(f"f{i}", wslice(ga[i] * 4, 2, xL), right_chip)
            pass_on(f"f{i}", wslice(ga[i] * 4 + 2, 2, xR), left_chip)

    def ring_done(i):
        if i:
            need(f"x{i}0r", f"x{i}1l", f"x{i}0l", f"x{i}1r", f"f{i}")
        else:
            need("xar", "xal", "x01r", "x01l", "f0")

    def task_sb(i):
        ring_done(i)
        cols = pl.ds(pl.multiple_of(c * HALF, HALF), HALF)
        for u in range(4):
            if i + u:
                send(f"sb{i}{u}", wg.at[ga[i] * 4 + gb[u], :, cols], wg.at[gb[u] * 4 + ga[i], :, cols], sibling)

    def task_m(i, u):
        need("cot")
        if i + u:
            ring_done(i)
            need(f"sb{u}{i}")
        else:
            need("w")
        cols = pl.ds(pl.multiple_of(fid(ga[i], gb[u]) * CH, CH), CH)
        grad_ref[:, cols] = dot_nt(cot_v[...], wg[ga[i] * 4 + gb[u]]).astype(BF16)

    tasks = {
        "w0": task_w0, "wf": task_wf, "xa": task_xa, "x01": task_x01,
        "gB0": functools.partial(task_block, "gB0", ("w",), a * 4 + b, 1, aB),
        "gB1": functools.partial(task_block, "gB1", ("wa",), a * 4 + bA, 1, aB),
        "gB2": functools.partial(task_block, "gB2", ("wb", "wf"), other_pair, 2, aB),
        "ga": functools.partial(task_group, "ga", ("wa", "wb", "wf"), a, aA),
        "gf": functools.partial(task_group, "gf", ("ga",), aA, aB),
        "q": task_q, "P0": functools.partial(left_terms, 0, 4), "P1": task_P1,
        "ph1": functools.partial(dp_exchange, "ph1", lambda peer: ppart.at[peer], rb1),
        "ph2": task_ph2, "ph3": task_ph3, "ph4": task_ph4,
        "GS": task_GS, "h0": task_h0, "h1": task_h1, "h2": task_h2,
        "ph5": functools.partial(a_exchange, "ph5", rb5), "ph6": task_ph6, "ph7": task_ph7,
        "base0": task_base0, "base1": lambda: approx(1, hacc[0, 0:8]),
        "tA": task_tA, "tB": task_tB,
        "E0b": functools.partial(task_E0, 1),
        "F00b": functools.partial(task_F0, "F00b", ("cot0b", "E0"), quarters[0], quarters[1]),
        "F00c": functools.partial(task_F0, "F00c", ("cot0b", "E0b"), quarters[1], halves[0]),
        "cot0": functools.partial(task_cot, "cot0", 0, 256),
        "cot0b": functools.partial(task_cot, "cot0b", 256, 256),
        "cot1": functools.partial(task_cot, "cot1", 512, 512),
    }
    for i in range(8):
        tasks[f"E{i}"] = functools.partial(task_E, i)
    for i in range(4):
        tasks[f"f{i}"] = functools.partial(task_f, i)
        tasks[f"sb{i}"] = functools.partial(task_sb, i)
        if i < 3:
            tasks[f"S{i}"] = functools.partial(task_S, i)
        for u in range(4):
            tasks[f"m{i}{u}"] = functools.partial(task_m, i, u)
        for u in range(2):
            tasks[f"F{i}{u}"] = functools.partial(task_F, i, u)
            if i:
                tasks[f"x{i}{u}"] = functools.partial(task_x, i, u)
    for u in range(2):
        tasks[f"b7{u}"] = functools.partial(task_b7, u)
        tasks[f"fin{u}"] = functools.partial(task_fin, u)

    tasks["E0"] = functools.partial(task_E0, 0)
    tasks["F00"] = functools.partial(task_F0, "F00", ("E0",), quarters[0], quarters[0])

    assert sorted(ORDER) == sorted(tasks)
    drained = 0
    first_fin = min(ORDER.index("fin0"), ORDER.index("fin1"))
    points = {ORDER.index("f3"): 40, ORDER.index("sb3"): 24, first_fin: 14}
    for place, name in enumerate(ORDER):
        if place in points:
            until = max(drained, len(sent) - points[place])
            for copy in sent[drained:until]:
                copy.wait_send()
            drained = until
        tasks[name]()

    need(*(name for name in flights))
    for copy in sent[drained:]:
        copy.wait_send()


N_WRITES = 4


def write_out(grad_v, new_v, right_v, grad_h, new_h, right_h, sem):
    rows = TOK // N_WRITES
    copies = [
        pltpu.make_async_copy(grad_v.at[pl.ds(i * rows, rows)], grad_h.at[pl.ds(i * rows, rows)], sem.at[i])
        for i in range(N_WRITES)
    ]
    copies.append(pltpu.make_async_copy(new_v, new_h, sem.at[N_WRITES]))
    copies.append(pltpu.make_async_copy(right_v, right_h, sem.at[N_WRITES + 1]))
    for copy in copies:
        copy.start()
    for copy in copies:
        copy.wait()


N_SEMS = 160


def shards(context, cotangent, out_weight, error_memory, seed_factor):
    vmem, hbm = pl.BlockSpec(memory_space=pltpu.VMEM), pl.BlockSpec(memory_space=pl.ANY)
    small = pltpu.VMEM((8, 8, 512), F32)
    quad = pltpu.VMEM((4, 8, 512), F32)
    results = pl.pallas_call(
        kernel,
        out_shape=(
            pltpu.VMEM((TOK, CH * N_FSDP), BF16),
            pltpu.VMEM((CH, D), BF16),
            pltpu.VMEM((4, D), F32),
        ),
        in_specs=[vmem, hbm, hbm, hbm, hbm],
        out_specs=(vmem, vmem, vmem),
        scratch_shapes=[
            pltpu.VMEM((N_FSDP, TOK, CH), BF16),
            pltpu.VMEM((TOK, D), BF16),
            pltpu.VMEM((CH, D), BF16),
            pltpu.VMEM((TOK, D), BF16),
            pltpu.VMEM((8, TOK, CH), BF16),
            pltpu.VMEM((4, CH, D), BF16),
            pltpu.VMEM((4, CH, D), BF16),
            pltpu.VMEM((3, CH, D), BF16),
            pltpu.VMEM((2, CUT, D), BF16),
            pltpu.VMEM((2, CH, D), BF16),
            pltpu.VMEM((N_FSDP, CH, D), BF16),
            pltpu.VMEM((CH, D), F32),
            small, small, quad, quad, small, small, quad, quad, small,
            pltpu.VMEM((2, 32, TOK), F32),
            pltpu.VMEM((8, CH), F32),
            pltpu.SemaphoreType.DMA((4,)),
            pltpu.SemaphoreType.DMA((N_SEMS,)),
            pltpu.SemaphoreType.DMA((N_SEMS,)),
        ],
        compiler_params=pltpu.CompilerParams(
            collective_id=0, has_side_effects=True, vmem_limit_bytes=52 * 2**20
        ),
        cost_estimate=pl.CostEstimate(flops=18 * 2**30, bytes_accessed=20 * 2**20, transcendentals=0),
        name="projection_gradient",
    )(seed_factor, cotangent, context, out_weight, error_memory[0])
    context_grad, new_memory, right_factor = pl.pallas_call(
        write_out,
        out_shape=tuple(jax.ShapeDtypeStruct(r.shape, r.dtype) for r in results),
        in_specs=[hbm] * 3,
        out_specs=(hbm,) * 3,
        scratch_shapes=[pltpu.SemaphoreType.DMA((N_WRITES + 2,))],
        cost_estimate=pl.CostEstimate(flops=0, bytes_accessed=9 * 2**20, transcendentals=0),
        compiler_params=pltpu.CompilerParams(vmem_limit_bytes=2**20),
        name="write_out",
    )(*(pltpu.with_memory_space_constraint(r, pltpu.VMEM) for r in results))
    return context_grad, new_memory[None], right_factor


def solution(mesh):
    placed = (
        P(("dp", "fsdp"), None),
        P(("dp", "fsdp"), None),
        P("fsdp", None),
        P("dp", "fsdp", None),
        P(),
    )
    return jax.shard_map(
        shards,
        mesh=mesh,
        in_specs=placed,
        out_specs=(P(("dp", "fsdp"), None), P("dp", "fsdp", None), P()),
        check_vma=False,
    )
```

```python
import functools

import jax
import jax.numpy as jnp
import numpy as np
from jax import lax
from jax.experimental import pallas as pl
from jax.experimental.pallas import tpu as pltpu
from jax.sharding import PartitionSpec as P

MESH = pl.DeviceIdType.MESH
F32 = jnp.float32
BF16 = jnp.bfloat16
EPSILON = 1e-06
TOK = 512
CH = 512
D = 1024
N_DP = 8
N_FSDP = 16
PIECE = 128
HALF = 512
SCALE = float(np.float32(1.0) / np.sqrt(np.float32(TOK * N_FSDP)))
CUT = 192
ORDER = (
    "w0", "q", "E1", "cot1", "gB0", "P0", "E0b", "xa", "wf", "P1", "ph1", "gB1", "x01", "gB2",
    "m00", "ph2", "E0", "ga", "cot0", "x10", "F11", "x11", "ph3", "F01", "ph4", "cot0b", "gf",
    "x20", "E2", "x21", "F00", "GS", "E4", "f1", "F10", "h0", "F00b", "f0", "h1", "h2", "F00c",
    "f2", "ph5", "E3", "E6", "F21", "sb1", "S0", "F30", "x30", "sb0", "E5", "ph6", "m01", "F20",
    "m11", "x31", "sb2", "F31", "E7", "m20", "m10", "m12", "m22", "m02", "m21", "ph7", "f3", "S1",
    "tA", "S2", "tB", "base0", "base1", "sb3", "m31", "m32", "b70", "m30", "m13", "b71", "m23",
    "m33", "fin0", "m03", "fin1",
)


def dot_tn(a, b):
    return lax.dot_general(a, b, (((0,), (0,)), ((), ())), preferred_element_type=F32)


def dot_nn(a, b):
    return lax.dot_general(a, b, (((1,), (0,)), ((), ())), preferred_element_type=F32)


def dot_nt(a, b):
    return lax.dot_general(a, b, (((1,), (1,)), ((), ())), preferred_element_type=F32)


def parts(v):
    hi = v.astype(BF16).astype(F32)
    rest = v - hi
    mid = rest.astype(BF16).astype(F32)
    return hi, mid, rest - mid


def stack(v):
    hi, mid, lo = parts(v)
    return jnp.concatenate([hi, mid, lo, jnp.zeros_like(hi)], axis=0).astype(BF16)


def fold(r):
    return r[0:8] + (r[8:16] + r[16:24])


def xor2(a, m):
    return ((a // 2 + m // 2) % 2) * 2 + (a % 2 + m % 2) % 2


def mask_of(i):
    return ((i + 1) % 3 + 1) * ((i + 2) // 3)


def kernel(
    seed_ref, cot_h, ctx_h, w_h, err_h,
    grad_ref, newmem_ref, right_ref,
    ctx_v, cot_v, err_v, cotp, ctxp, s1s, s1r, rsend, opp, fin, wg, base,
    ppart, rb1, rb2, rb3, pall, phat, rb5, rb6, rb7, hacc, p_own,
    lsem, ssem, rsem,
):
    dp, fs = lax.axis_index("dp"), lax.axis_index("fsdp")
    x, c = dp // 2, dp % 2
    z, y = fs // 4, fs % 4
    a, b = z * (1 - c) + y * c, y * (1 - c) + z * c

    def fid(i, j):
        return (i * (1 - c) + j * c) * 4 + j * (1 - c) + i * c

    def at(i, j):
        return (dp, fid(i, j))

    ga = [a, 3 - a, xor2(a, 1), xor2(a, 2)]
    gb = [b, 3 - b, xor2(b, 1), xor2(b, 2)]
    aB, aA, bB, bA = ga[1], ga[2], gb[1], gb[2]
    xR, xL = (x + 1) % 4, (x + 3) % 4
    right_chip, left_chip = (xR * 2 + c, fs), (xL * 2 + c, fs)
    sibling = (x * 2 + 1 - c, fs)
    border = [gb[3], bA, bB, b]
    row8 = lax.broadcasted_iota(jnp.int32, (8, CH), 0)
    mine8 = (row8 // 4) == (fs % 2)
    low, high = pl.ds(0, CUT), pl.ds(CUT, CH - CUT)
    halves = (pl.ds(0, HALF), pl.ds(HALF, HALF))

    barrier = pltpu.get_barrier_semaphore()
    peers = [((dp + i) % N_DP, fs) for i in range(1, N_DP)]
    peers += [at((a + i) % 4, b) for i in range(1, 4)]
    peers += [at(a, (b + i) % 4) for i in range(1, 4)]
    for peer in peers:
        pl.semaphore_signal(barrier, inc=1, device_id=peer, device_id_type=MESH)
    loads = {}

    def load(name, src, dst):
        loads[name] = pltpu.make_async_copy(src, dst, lsem.at[len(loads)])
        loads[name].start()

    load("cot", cot_h, cot_v)
    load("w", w_h, wg.at[a * 4 + b])
    for f in range(N_FSDP):
        pltpu.make_async_copy(ctx_h.at[:, pl.ds(f * CH, CH)], ctx_v.at[f], lsem.at[3]).start()
    load("err", err_h, err_v)
    loads["ctx"] = pltpu.make_async_copy(ctx_v, ctx_v, lsem.at[3])

    pl.semaphore_wait(barrier, len(peers))

    sent, flights, arrived = [], {}, set()

    def send(name, src, dst, device):
        n = len(sent)
        copy = pltpu.make_async_remote_copy(src, dst, ssem.at[n], rsem.at[n], device_id=device, device_id_type=MESH)
        copy.start()
        sent.append(copy)
        flights.setdefault(name, []).append(copy)

    def need(*names):
        for name in names:
            if name in loads:
                loads.pop(name).wait()
            elif name in flights and name not in arrived:
                arrived.add(name)
                for copy in flights[name]:
                    copy.wait_recv()
            else:
                assert name in arrived or name in ("cot", "w", "err", "ctx"), name

    def dp_exchange(name, src_of, buf):
        for i in range(1, N_DP):
            send(name, src_of((dp + i) % N_DP), buf.at[dp], ((dp + i) % N_DP, fs))

    def a_exchange(name, buf):
        for i in range(1, 4):
            send(name, buf.at[a], buf.at[a], at((a + i) % 4, b))

    def b_exchange(name, buf):
        for i in range(1, 4):
            send(name, buf.at[b], buf.at[b], at(a, (b + i) % 4))

    def total(buf, n):
        t = buf[0]
        for i in range(1, n):
            t = t + buf[i]
        return t

    def task_q():
        need("cot")
        seed32 = stack(jnp.concatenate([seed_ref[...], seed_ref[...]], axis=0))
        hacc[0] = dot_nt(seed32, cot_v[...])
        need("err")
        p_own[...] = jnp.where(mine8, fold(dot_nt(seed32, err_v[...])), 0.0)

    def left_terms(first, last):
        need("ctx")
        q32 = stack(fold(hacc[0]))

        def step(s, carry):
            even = fold(dot_nn(q32, ctx_v[2 * s]))
            odd = fold(dot_nn(q32, ctx_v[2 * s + 1]))
            ppart[s] = jnp.where(row8 < 4, even, odd) * SCALE
            return carry

        lax.fori_loop(first, last, step, 0)

    def task_P1():
        left_terms(4, 8)
        ppart[fs // 2] = ppart[fs // 2] + p_own[...]
        rb1[dp] = ppart[dp]

    def task_ph2():
        need("ph1")
        rb2[a] = total(rb1, N_DP)
        a_exchange("ph2", rb2)

    def task_ph3():
        need("ph2")
        rb3[b] = total(rb2, 4)
        b_exchange("ph3", rb3)

    def task_ph4():
        need("ph3")
        pall[dp] = total(rb3, 4)
        dp_exchange("ph4", lambda peer: pall.at[dp], pall)

    def inner(u, v):
        t = u[0] * v[0] + u[1] * v[1]
        return jnp.sum(jnp.sum(t, axis=1, keepdims=True), axis=0, keepdims=True)

    def task_GS():
        need("ph4")
        basis = []
        for j in range(4):
            v = (pall[:, j, :], pall[:, j + 4, :])
            if j:
                coeffs = [inner(q, v) for q in basis]
                cut0 = coeffs[0] * basis[0][0]
                cut1 = coeffs[0] * basis[0][1]
                for k in range(1, j):
                    cut0 = cut0 + coeffs[k] * basis[k][0]
                    cut1 = cut1 + coeffs[k] * basis[k][1]
                v = (v[0] - cut0, v[1] - cut1)
            length = jnp.sqrt(inner(v, v) + EPSILON)
            v = (v[0] / length, v[1] / length)
            basis.append(v)
            phat[:, j, :] = v[0]
            phat[:, j + 4, :] = v[1]

    def rows_terms(first, last):
        def step(s, carry):
            p32 = stack(phat[s])
            return carry[0] + dot_nt(p32, ctx_v[2 * s]), carry[1] + dot_nt(p32, ctx_v[2 * s + 1])

        return lax.fori_loop(first, last, step, (hacc[0], hacc[1]))

    def task_h0():
        hacc[...] = jnp.zeros_like(hacc)
        hacc[0], hacc[1] = rows_terms(0, 4)

    def task_h1():
        hacc[0], hacc[1] = rows_terms(4, 8)

    def task_h2():
        mix = jnp.where(row8 < 4, fold(hacc[0]), fold(hacc[1]))
        h8 = mix + jnp.concatenate([mix[4:8], mix[0:4]], axis=0)
        slot_rows = phat[fs // 2]
        turned = jnp.concatenate([slot_rows[4:8], slot_rows[0:4]], axis=0)
        p8 = jnp.where(mine8, slot_rows, turned)
        p_own[...] = p8
        r8 = fold(dot_nn(stack(h8), cot_v[...])) * SCALE + fold(dot_nn(stack(p8), err_v[...]))
        rb5[a] = jnp.where(row8 < 4, r8[:, 0:512], r8[:, 512:1024])

    def task_ph6():
        need("ph5")
        rb6[b] = total(rb5, 4)
        b_exchange("ph6", rb6)

    def task_ph7():
        need("ph6")
        rb7[dp] = total(rb6, 4)
        dp_exchange("ph7", lambda peer: rb7.at[dp], rb7)

    def approx(half, factor):
        ph, pm, plo = parts(p_own[...])
        rh, rm, rl = parts(jnp.where((row8 // 4) == half, factor, 0.0))
        lhs = jnp.concatenate([ph, ph, pm, ph, plo, pm], axis=0).astype(BF16)
        rhs = jnp.concatenate([rh, rm, rh, rl, rh, rm], axis=0).astype(BF16)
        base[:, halves[half]] = err_v[:, halves[half]].astype(F32) - dot_tn(lhs, rhs)

    def task_base0():
        need("ph7")
        factor = total(rb7, N_DP) * (1.0 / N_DP)
        hacc[0, 0:8] = factor
        right_ref[:, 0:512] = factor[0:4]
        right_ref[:, 512:1024] = factor[4:8]
        approx(0, factor)

    def task_cot(name, first, count):
        cols = pl.ds(first, count)
        send(name, cot_h.at[:, cols], cotp.at[:, cols], at(aA, b))

    quarters = (pl.ds(0, 256), pl.ds(256, 256))

    def task_E(j):
        need("ctx")
        send(f"E{j}", ctx_v.at[fid(3 - aA if j < 4 else aA, border[j % 4])], ctxp.at[j], at(aA, b))

    def task_E0(part):
        need("ctx")
        cols = quarters[part]
        send(("E0", "E0b")[part], ctx_v.at[fid(3 - aA, border[0]), :, cols], ctxp.at[0, :, cols], at(aA, b))

    def product(f, j, cols=slice(None), rows=slice(None)):
        return dot_tn(ctx_v[f, :, rows], cot_v[:, cols]) + dot_tn(ctxp[j, :, rows], cotp[:, cols])

    def task_F(k, half):
        need("cot", f"E{k}", *(("cot0", "cot0b") if half == 0 else ("cot1",)))
        if k == 0:
            need("E0b")
        cols = halves[half]
        s1s[k, :, cols] = product(fid(aB, border[k]), k, cols).astype(BF16)
        send(f"F{k}{half}", s1s.at[k, :, cols], s1r.at[k, :, cols], at(aB, b))

    def task_F0(name, needed, rows, cols):
        need("cot", "cot0", *needed)
        s1s[0, rows, cols] = product(fid(aB, border[0]), 0, cols, rows).astype(BF16)
        send(name, s1s.at[0, rows, cols], s1r.at[0, rows, cols], at(aB, b))

    def task_S(k):
        need(f"E{4 + k}", f"F{k}0", f"F{k}1", "cot0", "cot0b", "cot1")
        if k == 0:
            need("F00b", "F00c")
        rsend[k] = (product(fid(a, border[k]), 4 + k) + s1r[k].astype(F32)).astype(BF16)
        if k == 0:
            send("oB", rsend.at[0, low], opp.at[0, pl.ds(0, CUT)], at(a, bB))
            send("oA", rsend.at[0, high], opp.at[1, pl.ds(0, CH - CUT)], at(a, bA))
        elif k == 1:
            send("dA", rsend.at[1, high], fin.at[0, high], at(a, bA))
        else:
            send("dB", rsend.at[2, low], fin.at[1, low], at(a, bB))

    def task_tA():
        need("oB")
        rsend[1, low] = (rsend[1, low].astype(F32) + opp[0, 0:CUT].astype(F32)).astype(BF16)
        send("tA", rsend.at[1, low], fin.at[0, low], at(a, bA))

    def task_tB():
        need("oA")
        rsend[2, high] = (rsend[2, high].astype(F32) + opp[1, 0:CH - CUT].astype(F32)).astype(BF16)
        send("tB", rsend.at[2, high], fin.at[1, high], at(a, bB))

    def task_b7(half):
        need("E7", "cot0", "cot0b", "cot1")
        base[:, halves[half]] += product(fid(a, b), 7, halves[half]) * SCALE

    def task_fin(half):
        need("F30", "F31", *(("tA", "dB") if half == 0 else ("dA", "tB")))
        rows = (low, high)[half]
        gathered = s1r[3, rows].astype(F32) + (fin[0, rows].astype(F32) + fin[1, rows].astype(F32))
        newmem_ref[rows, :] = (base[rows, :] + gathered * SCALE).astype(BF16)

    def wslice(first, count, slot, rows=PIECE, shift=0):
        return wg.at[
            pl.ds(first, count),
            pl.ds(pl.multiple_of(slot * PIECE + shift, rows), rows),
            pl.ds(pl.multiple_of(c * HALF, HALF), HALF),
        ]

    def pass_on(name, src, device):
        send(name, src, src, device)

    def task_w0():
        need("w")
        pass_on("wa", wslice(a * 4 + b, 1, x), at(a, bA))
        pass_on("wb", wslice(a * 4 + b, 1, x), at(a, bB))

    def task_wf():
        need("wa")
        pass_on("wf", wslice(a * 4 + bA, 1, x), at(a, bB))

    def task_group(name, needed, source, target):
        need(*needed)
        pass_on(name, wslice(source * 4, 4, x), at(target, b))

    def task_block(name, needed, first, count, target):
        need(*needed)
        pass_on(name, wslice(first, count, x), at(target, b))

    def both(name, first, count):
        pass_on(name + "r", wslice(first, count, x), right_chip)
        pass_on(name + "l", wslice(first, count, x), left_chip)

    def task_xa():
        need("wa")
        both("xa", a * 4 + bA, 1)

    other_pair = a * 4 + (1 - b // 2) * 2

    def task_x01():
        need("wb", "wf")
        both("x01", other_pair, 2)

    def task_x(i, part):
        need(*((), ("gB0", "gB1", "gB2"), ("ga",), ("gf",))[i])
        both(f"x{i}{part}", ga[i] * 4 + part * 2, 2)

    def task_f(i):
        if i == 0:
            need("xar", "xal", "x01r", "x01l")
            pass_on("f0", wslice(a * 4 + bA, 1, xL, 64, 0), right_chip)
            pass_on("f0", wslice(a * 4 + bA, 1, xR, 64, 64), left_chip)
            pass_on("f0", wslice(other_pair, 1, xL), right_chip)
            pass_on("f0", wslice(other_pair + 1, 1, xR), left_chip)
        else:
            need(f"x{i}0r", f"x{i}1l")
            pass_on(f"f{i}", wslice(ga[i] * 4, 2, xL), right_chip)
            pass_on(f"f{i}", wslice(ga[i] * 4 + 2, 2, xR), left_chip)

    def ring_done(i):
        if i:
            need(f"x{i}0r", f"x{i}1l", f"x{i}0l", f"x{i}1r", f"f{i}")
        else:
            need("xar", "xal", "x01r", "x01l", "f0")

    def task_sb(i):
        ring_done(i)
        cols = pl.ds(pl.multiple_of(c * HALF, HALF), HALF)
        for u in range(4):
            if i + u:
                send(f"sb{i}{u}", wg.at[ga[i] * 4 + gb[u], :, cols], wg.at[gb[u] * 4 + ga[i], :, cols], sibling)

    def task_m(i, u):
        need("cot")
        if i + u:
            ring_done(i)
            need(f"sb{u}{i}")
        else:
            need("w")
        cols = pl.ds(pl.multiple_of(fid(ga[i], gb[u]) * CH, CH), CH)
        grad_ref[:, cols] = dot_nt(cot_v[...], wg[ga[i] * 4 + gb[u]]).astype(BF16)

    tasks = {
        "w0": task_w0, "wf": task_wf, "xa": task_xa, "x01": task_x01,
        "gB0": functools.partial(task_block, "gB0", ("w",), a * 4 + b, 1, aB),
        "gB1": functools.partial(task_block, "gB1", ("wa",), a * 4 + bA, 1, aB),
        "gB2": functools.partial(task_block, "gB2", ("wb", "wf"), other_pair, 2, aB),
        "ga": functools.partial(task_group, "ga", ("wa", "wb", "wf"), a, aA),
        "gf": functools.partial(task_group, "gf", ("ga",), aA, aB),
        "q": task_q, "P0": functools.partial(left_terms, 0, 4), "P1": task_P1,
        "ph1": functools.partial(dp_exchange, "ph1", lambda peer: ppart.at[peer], rb1),
        "ph2": task_ph2, "ph3": task_ph3, "ph4": task_ph4,
        "GS": task_GS, "h0": task_h0, "h1": task_h1, "h2": task_h2,
        "ph5": functools.partial(a_exchange, "ph5", rb5), "ph6": task_ph6, "ph7": task_ph7,
        "base0": task_base0, "base1": lambda: approx(1, hacc[0, 0:8]),
        "tA": task_tA, "tB": task_tB,
        "E0b": functools.partial(task_E0, 1),
        "F00b": functools.partial(task_F0, "F00b", ("cot0b", "E0"), quarters[0], quarters[1]),
        "F00c": functools.partial(task_F0, "F00c", ("cot0b", "E0b"), quarters[1], halves[0]),
        "cot0": functools.partial(task_cot, "cot0", 0, 256),
        "cot0b": functools.partial(task_cot, "cot0b", 256, 256),
        "cot1": functools.partial(task_cot, "cot1", 512, 512),
    }
    for i in range(8):
        tasks[f"E{i}"] = functools.partial(task_E, i)
    for i in range(4):
        tasks[f"f{i}"] = functools.partial(task_f, i)
        tasks[f"sb{i}"] = functools.partial(task_sb, i)
        if i < 3:
            tasks[f"S{i}"] = functools.partial(task_S, i)
        for u in range(4):
            tasks[f"m{i}{u}"] = functools.partial(task_m, i, u)
        for u in range(2):
            tasks[f"F{i}{u}"] = functools.partial(task_F, i, u)
            if i:
                tasks[f"x{i}{u}"] = functools.partial(task_x, i, u)
    for u in range(2):
        tasks[f"b7{u}"] = functools.partial(task_b7, u)
        tasks[f"fin{u}"] = functools.partial(task_fin, u)

    tasks["E0"] = functools.partial(task_E0, 0)
    tasks["F00"] = functools.partial(task_F0, "F00", ("E0",), quarters[0], quarters[0])

    assert sorted(ORDER) == sorted(tasks)
    drained = 0
    first_fin = min(ORDER.index("fin0"), ORDER.index("fin1"))
    points = {ORDER.index("f3"): 40, ORDER.index("sb3"): 24, first_fin: 14}
    for place, name in enumerate(ORDER):
        if place in points:
            until = max(drained, len(sent) - points[place])
            for copy in sent[drained:until]:
                copy.wait_send()
            drained = until
        tasks[name]()

    need(*(name for name in flights))
    for copy in sent[drained:]:
        copy.wait_send()


N_WRITES = 4


def write_out(grad_v, new_v, right_v, grad_h, new_h, right_h, sem):
    rows = TOK // N_WRITES
    copies = [
        pltpu.make_async_copy(grad_v.at[pl.ds(i * rows, rows)], grad_h.at[pl.ds(i * rows, rows)], sem.at[i])
        for i in range(N_WRITES)
    ]
    copies.append(pltpu.make_async_copy(new_v, new_h, sem.at[N_WRITES]))
    copies.append(pltpu.make_async_copy(right_v, right_h, sem.at[N_WRITES + 1]))
    for copy in copies:
        copy.start()
    for copy in copies:
        copy.wait()


N_SEMS = 160


def shards(context, cotangent, out_weight, error_memory, seed_factor):
    vmem, hbm = pl.BlockSpec(memory_space=pltpu.VMEM), pl.BlockSpec(memory_space=pl.ANY)
    small = pltpu.VMEM((8, 8, 512), F32)
    quad = pltpu.VMEM((4, 8, 512), F32)
    results = pl.pallas_call(
        kernel,
        out_shape=(
            pltpu.VMEM((TOK, CH * N_FSDP), BF16),
            pltpu.VMEM((CH, D), BF16),
            pltpu.VMEM((4, D), F32),
        ),
        in_specs=[vmem, hbm, hbm, hbm, hbm],
        out_specs=(vmem, vmem, vmem),
        scratch_shapes=[
            pltpu.VMEM((N_FSDP, TOK, CH), BF16),
            pltpu.VMEM((TOK, D), BF16),
            pltpu.VMEM((CH, D), BF16),
            pltpu.VMEM((TOK, D), BF16),
            pltpu.VMEM((8, TOK, CH), BF16),
            pltpu.VMEM((4, CH, D), BF16),
            pltpu.VMEM((4, CH, D), BF16),
            pltpu.VMEM((3, CH, D), BF16),
            pltpu.VMEM((2, max(CUT, CH - CUT), D), BF16),
            pltpu.VMEM((2, CH, D), BF16),
            pltpu.VMEM((N_FSDP, CH, D), BF16),
            pltpu.VMEM((CH, D), F32),
            small, small, quad, quad, small, small, quad, quad, small,
            pltpu.VMEM((2, 32, TOK), F32),
            pltpu.VMEM((8, CH), F32),
            pltpu.SemaphoreType.DMA((4,)),
            pltpu.SemaphoreType.DMA((N_SEMS,)),
            pltpu.SemaphoreType.DMA((N_SEMS,)),
        ],
        compiler_params=pltpu.CompilerParams(
            collective_id=0, has_side_effects=True, vmem_limit_bytes=52 * 2**20
        ),
        cost_estimate=pl.CostEstimate(flops=18 * 2**30, bytes_accessed=20 * 2**20, transcendentals=0),
        name="projection_gradient",
    )(seed_factor, cotangent, context, out_weight, error_memory[0])
    context_grad, new_memory, right_factor = pl.pallas_call(
        write_out,
        out_shape=tuple(jax.ShapeDtypeStruct(r.shape, r.dtype) for r in results),
        in_specs=[hbm] * 3,
        out_specs=(hbm,) * 3,
        scratch_shapes=[pltpu.SemaphoreType.DMA((N_WRITES + 2,))],
        cost_estimate=pl.CostEstimate(flops=0, bytes_accessed=9 * 2**20, transcendentals=0),
        compiler_params=pltpu.CompilerParams(vmem_limit_bytes=2**20),
        name="write_out",
    )(*(pltpu.with_memory_space_constraint(r, pltpu.VMEM) for r in results))
    return context_grad, new_memory[None], right_factor


def solution(mesh):
    placed = (
        P(("dp", "fsdp"), None),
        P(("dp", "fsdp"), None),
        P("fsdp", None),
        P("dp", "fsdp", None),
        P(),
    )
    return jax.shard_map(
        shards,
        mesh=mesh,
        in_specs=placed,
        out_specs=(P(("dp", "fsdp"), None), P("dp", "fsdp", None), P()),
        check_vma=False,
    )
```
